32 devices in a mesh: dp: 2 (over x), row: 4 (over z), col: 4 (over y, core).
Axes of the slice: x: 2, y: 2, z: 4, core: 2. Of those that a mesh axis runs over, the one named last changes fastest.
Arguments:
- query_out: bfloat16 [384, 4096], P(('dp', 'row'), 'col'), may hold values from -6 to 6
- query_in: bfloat16 [384, 4096], P(('dp', 'col')), may hold values from -6 to 6
- out_basis: bfloat16 [4096, 4096], P('col', ('dp', 'row')), may hold values from -0.09375 to 0.09375
- in_basis: bfloat16 [4096, 4096], P(('dp', 'row'), 'col'), may hold values from -0.09375 to 0.09375
- eigvals: float32 [4096, 4096], P(('dp', 'row'), 'col'), may hold values from 16 to 1024
- train_out: bfloat16 [384, 4096], P(('dp', 'row'), 'col'), may hold values from -0.09375 to 0.09375
- train_in: bfloat16 [384, 4096], P(('dp', 'col')), may hold values from -0.09375 to 0.09375
Outputs:
- precond: float32 [4096, 4096], P(('dp', 'row'), 'col')
- scores: float32 [384], P('dp')
The draws below stay inside these ranges and needn't reach their ends.
All inputs are finite; a program needn't handle non-finite values.
Results may differ from the reference program's by a relative error of at most 0.028.
Values may be sent and summed in bfloat16 or wider, within the bound.
A program may use at most 64 MiB of HBM per device.

```python
import math
import jax
import jax.numpy as jnp
from jax import lax

DO = 4096
DI = 4096
TOK_DEV = 192
TOKENS = 384
N_DP = 2
N_ROW = 4
N_COL = 4


def levels(rng, extent, cuts, smallest, high):
    def one(axis_at, shards_of):
        heights = jax.random.uniform(jax.random.fold_in(jax.random.fold_in(rng, 6), axis_at), (shards_of,), jnp.float32, smallest / len(cuts), high / len(cuts))
        return jnp.repeat(jnp.exp(heights), extent[axis_at] // shards_of).reshape((-1,) + (1,) * (len(extent) - axis_at - 1))

    factor_of = one(*cuts[0])
    for cut in cuts[1:]:
        factor_of = factor_of * one(*cut)
    return factor_of


def gaussian(own_key, dims, deviation, limit, split=(), held_as=jnp.bfloat16):
    result = deviation * jax.random.normal(own_key, dims, jnp.float32)
    if split:
        result = result * levels(own_key, dims, split, -0.22, 0.18)
    return jnp.clip(result, -limit, limit).astype(held_as)


def setup_inputs(seed: int = 0) -> dict:
    streams_of = jax.random.split(jax.random.key(seed), 8)
    query_out = gaussian(streams_of[0], (TOKENS, DO), 1.0, 6.0, ((0, 8), (1, 4)))
    query_in = gaussian(streams_of[1], (TOKENS, DI), 1.0, 6.0, ((0, 8),))
    out_basis = gaussian(streams_of[2], (DO, DO), DO ** -0.5, 0.09375, ((0, 4), (1, 8)))
    in_basis = gaussian(streams_of[3], (DI, DI), DI ** -0.5, 0.09375, ((0, 8), (1, 4)))
    eigvals = jnp.clip(jnp.exp(math.log(1024.0) - 4.158883 * jax.random.uniform(streams_of[4], (DO, DI), jnp.float32) ** levels(streams_of[4], (DO, DI), ((0, 8), (1, 4)), -0.2, 0.2)), 16.0, 1024.0)
    train_out = gaussian(streams_of[5], (TOKENS, DO), 0.015625, 0.09375, ((0, 8), (1, 4)))
    train_in = gaussian(streams_of[6], (TOKENS, DI), 0.015625, 0.09375, ((0, 8),))
    return dict(query_out=query_out, query_in=query_in, out_basis=out_basis, in_basis=in_basis, eigvals=eigvals, train_out=train_out, train_in=train_in)


damping = 1.0


def rounded(value):
    return lax.optimization_barrier(value.astype(jnp.bfloat16)).astype(jnp.float32)


def rotate_out(tok_rows, basis):
    width = DO // N_COL
    summed = jnp.zeros((tok_rows.shape[0], DO), jnp.float32)
    for block in range(N_COL):
        partial_sum = jnp.dot(tok_rows[:, block * width:(block + 1) * width], basis[block * width:(block + 1) * width], preferred_element_type=jnp.float32)
        summed = summed + rounded(partial_sum)
    return summed.astype(jnp.bfloat16)


def rotate_in(tok_rows, basis):
    sub_width = DI // (N_DP * N_ROW)
    count_rows = tok_rows.shape[0]
    split_rows = tok_rows.reshape(count_rows, N_DP, N_ROW, sub_width)
    split_basis = basis.reshape(N_DP, N_ROW, sub_width, DI)
    summed = jnp.zeros((count_rows, DI), jnp.float32)
    for block in range(N_ROW):
        picked = split_rows[:, :, block, :].reshape(count_rows, N_DP * sub_width)
        panel_rows = split_basis[:, block].reshape(N_DP * sub_width, DI)
        partial_sum = jnp.dot(picked, panel_rows, preferred_element_type=jnp.float32)
        summed = summed + rounded(partial_sum)
    return summed.astype(jnp.bfloat16)


def reference(query_out, query_in, out_basis, in_basis, eigvals, train_out, train_in):
    query_rot = rotate_out(query_out, out_basis).reshape(N_DP, TOK_DEV, DO)
    query_inr = rotate_in(query_in, in_basis).reshape(N_DP, TOK_DEV, DI)

    def add_group(summed, pair):
        left_part, right_part = pair
        partial_sum = lax.dot_general(left_part, right_part, (((0,), (0,)), ((), ())), preferred_element_type=jnp.float32)
        return summed + rounded(partial_sum), None

    grad, _ = lax.scan(add_group, jnp.zeros((DO, DI), jnp.float32), (query_rot, query_inr))
    precond = grad / (eigvals + damping)
    shared = precond.astype(jnp.bfloat16)
    train_rot = rotate_out(train_out, out_basis)
    train_inr = rotate_in(train_in, in_basis)
    mixed = jnp.dot(train_rot, shared, preferred_element_type=jnp.float32)
    scores = jnp.sum(mixed * train_inr.astype(jnp.float32), axis=1)
    return precond, scores
```

```python
import jax
import jax.numpy as jnp
from jax import lax
from jax.sharding import PartitionSpec as P

damping = 1.0


def rotate_out(tok_rows, basis_panel):
    gathered = lax.all_gather(tok_rows, "row", axis=0, tiled=True)
    partial_sum = jnp.dot(gathered, basis_panel, preferred_element_type=jnp.float32)
    return lax.psum(partial_sum.astype(jnp.bfloat16), "col")


def rotate_in(tok_rows, basis_panel):
    groups = lax.axis_size("dp")
    row_count = lax.axis_size("row")
    sub_width = tok_rows.shape[1] // (groups * row_count)
    split_rows = tok_rows.reshape(tok_rows.shape[0], groups, row_count, sub_width)
    picked = lax.dynamic_index_in_dim(split_rows, lax.axis_index("row"), 2, keepdims=False)
    picked = picked.reshape(tok_rows.shape[0], groups * sub_width)
    gathered = lax.all_gather(picked, "col", axis=0, tiled=True)
    partial_sum = jnp.dot(gathered, basis_panel, preferred_element_type=jnp.float32)
    return lax.psum(partial_sum.astype(jnp.bfloat16), "row")


def wide_plan(query_out, query_in, out_basis, in_basis, eigvals, train_out, train_in):
    panel_out = lax.all_gather(out_basis, "dp", axis=1, tiled=True)
    panel_in = lax.all_gather(in_basis, "dp", axis=0, tiled=True)
    query_rot = rotate_out(query_out, panel_out)
    query_inr = rotate_in(query_in, panel_in)
    partial_grad = lax.dot_general(
        query_rot, query_inr, (((0,), (0,)), ((), ())), preferred_element_type=jnp.float32
    )
    owned = lax.psum_scatter(
        partial_grad.astype(jnp.bfloat16), "dp", scatter_dimension=0, tiled=True
    ).astype(jnp.float32)
    precond = owned / (eigvals + damping)
    shared = precond.astype(jnp.bfloat16)
    train_rot = rotate_out(train_out, panel_out)
    train_inr = rotate_in(train_in, panel_in)
    mixed = jnp.dot(
        train_rot,
        lax.all_gather(shared, "dp", axis=0, tiled=True),
        preferred_element_type=jnp.float32,
    )
    partial_scores = jnp.sum(mixed * train_inr.astype(jnp.float32), axis=1)
    scores = lax.psum(partial_scores, ("row", "col"))
    return (precond, scores)


def local_plan(query_out, query_in, out_basis, in_basis, eigvals, train_out, train_in):
    groups = lax.axis_size("dp")
    row_count = lax.axis_size("row")
    own = query_out.shape[0]
    stacked = jnp.stack([query_out, train_out])
    out_rows = lax.all_gather(stacked, ("dp", "row"), axis=1, tiled=True)
    sub_width = query_in.shape[1] // (groups * row_count)
    in_stack = jnp.stack([query_in, train_in]).reshape(2, own, groups, row_count, sub_width)
    picked = lax.dynamic_index_in_dim(in_stack, lax.axis_index("row"), 3, keepdims=False)
    in_rows = lax.all_gather(picked, ("dp", "col"), axis=1, tiled=True)
    in_rows = lax.dynamic_index_in_dim(in_rows, lax.axis_index("dp"), 2, keepdims=False)
    tokens = out_rows.shape[1]
    out_part = jnp.dot(out_rows.reshape(2 * tokens, -1), out_basis, preferred_element_type=jnp.float32)
    in_part = jnp.dot(in_rows.reshape(2 * tokens, -1), in_basis, preferred_element_type=jnp.float32)
    rot = lax.psum(out_part.astype(jnp.bfloat16), "col")
    inr = lax.psum(in_part.astype(jnp.bfloat16), ("dp", "row"))
    grad = lax.dot_general(
        rot[:tokens], inr[:tokens], (((0,), (0,)), ((), ())), preferred_element_type=jnp.float32
    )
    precond = grad / (eigvals + damping)
    mixed = jnp.dot(rot[tokens:], precond.astype(jnp.bfloat16), preferred_element_type=jnp.float32)
    partial_scores = jnp.sum(mixed * inr[tokens:].astype(jnp.float32), axis=1)
    total = lax.psum(partial_scores, ("dp", "row", "col"))
    kept = tokens // groups
    return (precond, lax.dynamic_slice_in_dim(total, lax.axis_index("dp") * kept, kept))


def solution(mesh):
    in_specs = (
        P(("dp", "row"), "col"),
        P(("dp", "col"), None),
        P("col", ("dp", "row")),
        P(("dp", "row"), "col"),
        P(("dp", "row"), "col"),
        P(("dp", "row"), "col"),
        P(("dp", "col"), None),
    )
    out_specs = (P(("dp", "row"), "col"), P("dp"))
    return jax.shard_map(
        local_plan if mesh.shape["dp"] <= 2 else wide_plan, mesh=mesh, in_specs=in_specs, out_specs=out_specs, check_vma=False
    )
```

```python
import functools

import jax
import jax.numpy as jnp
from jax import lax
from jax.experimental import pallas as pl
from jax.experimental.pallas import tpu as pltpu
from jax.sharding import PartitionSpec as P

damping = 1.0


def rotate_out(tok_rows, basis_panel):
    gathered = lax.all_gather(tok_rows, "row", axis=0, tiled=True)
    partial_sum = jnp.dot(gathered, basis_panel, preferred_element_type=jnp.float32)
    return lax.psum(partial_sum.astype(jnp.bfloat16), "col")


def rotate_in(tok_rows, basis_panel):
    groups = lax.axis_size("dp")
    row_count = lax.axis_size("row")
    sub_width = tok_rows.shape[1] // (groups * row_count)
    split_rows = tok_rows.reshape(tok_rows.shape[0], groups, row_count, sub_width)
    picked = lax.dynamic_index_in_dim(split_rows, lax.axis_index("row"), 2, keepdims=False)
    picked = picked.reshape(tok_rows.shape[0], groups * sub_width)
    gathered = lax.all_gather(picked, "col", axis=0, tiled=True)
    partial_sum = jnp.dot(gathered, basis_panel, preferred_element_type=jnp.float32)
    return lax.psum(partial_sum.astype(jnp.bfloat16), "row")


def wide_plan(query_out, query_in, out_basis, in_basis, eigvals, train_out, train_in):
    panel_out = lax.all_gather(out_basis, "dp", axis=1, tiled=True)
    panel_in = lax.all_gather(in_basis, "dp", axis=0, tiled=True)
    query_rot = rotate_out(query_out, panel_out)
    query_inr = rotate_in(query_in, panel_in)
    partial_grad = lax.dot_general(
        query_rot, query_inr, (((0,), (0,)), ((), ())), preferred_element_type=jnp.float32
    )
    owned = lax.psum_scatter(
        partial_grad.astype(jnp.bfloat16), "dp", scatter_dimension=0, tiled=True
    ).astype(jnp.float32)
    precond = owned / (eigvals + damping)
    shared = precond.astype(jnp.bfloat16)
    train_rot = rotate_out(train_out, panel_out)
    train_inr = rotate_in(train_in, panel_in)
    mixed = jnp.dot(
        train_rot,
        lax.all_gather(shared, "dp", axis=0, tiled=True),
        preferred_element_type=jnp.float32,
    )
    partial_scores = jnp.sum(mixed * train_inr.astype(jnp.float32), axis=1)
    scores = lax.psum(partial_scores, ("row", "col"))
    return (precond, scores)


bf16 = jnp.bfloat16
f32 = jnp.float32


def dot(left, right):
    return jnp.dot(left, right, preferred_element_type=f32)


def flat(block):
    return block.reshape(-1, block.shape[-1])


def kernel(
    q_out, q_in, basis_out_hbm, basis_in_hbm, eig_hbm, t_out, t_in,
    precond, scores,
    basis_out, basis_in, eig, tin, pin, xr, zs, zr, fin, tout, pout, sr, ys, yr, rot,
    part, col_sc, row_sc, dp_sc,
    local_sem, send_sem, tin_sem, xr_sem, zr_sem, fin_sem, tout_sem, out_sem, sc_sem,
):
    d, r, c = lax.axis_index("dp"), lax.axis_index("row"), lax.axis_index("col")
    e = 1 - d
    core = lax.rem(c, 2)
    sib = c + 1 - 2 * core
    far = lax.rem(c + 2, 4)
    sibling, across, other, diagonal = (d, r, sib), (d, r, far), (e, r, c), (e, r, far)
    rows = [lax.rem(r + k, 4) for k in (1, 2, 3)]
    cols = [lax.rem(c + k, 4) for k in (1, 2, 3)]
    own_out, own_in = 4 * d + r, 4 * d + c
    toks, outs = (q_in, t_in), (q_out, t_out)
    width = basis_in.shape[0]

    loads = [
        pltpu.make_async_copy(basis_in_hbm, basis_in, local_sem.at[0]),
        pltpu.make_async_copy(basis_out_hbm, basis_out, local_sem.at[1]),
        pltpu.make_async_copy(eig_hbm, eig, local_sem.at[2]),
    ]
    for load in loads:
        load.start()

    barrier = pltpu.get_barrier_semaphore()
    peers = [(d, r, j) for j in cols] + [(d, j, c) for j in rows] + [other, diagonal]
    for peer in peers:
        pl.semaphore_signal(barrier, inc=1, device_id=peer, device_id_type=pl.DeviceIdType.MESH)
    pl.semaphore_wait(barrier, len(peers))

    sends = []

    def send(src, dst, sem, peer):
        copy = pltpu.make_async_remote_copy(
            src_ref=src, dst_ref=dst, send_sem=send_sem.at[len(sends)], recv_sem=sem,
            device_id=peer, device_id_type=pl.DeviceIdType.MESH,
        )
        copy.start()
        sends.append(copy)

    def got(dst, sem):
        pltpu.make_async_remote_copy(
            src_ref=dst, dst_ref=dst, send_sem=send_sem.at[0], recv_sem=sem,
            device_id=sibling, device_id_type=pl.DeviceIdType.MESH,
        ).wait_recv()

    def columns(ref, group):
        return ref.at[:, pl.ds(pl.multiple_of((group * 4 + r) * width, width), width)]

    mine = []
    for ch in range(2):
        for peer in (other, across, diagonal, sibling):
            send(columns(toks[ch], peer[0]), tin.at[ch, own_in], tin_sem.at[ch, own_in], peer)
        keep = pltpu.make_async_copy(columns(toks[ch], d), tin.at[ch, own_in], local_sem.at[3 + ch])
        keep.start()
        mine.append(keep)
    for ch in range(2):
        for j in rows:
            send(outs[ch], tout.at[ch, own_out], tout_sem.at[ch, own_out], (d, j, c))
        send(outs[ch], tout.at[ch, own_out], tout_sem.at[ch, own_out], other)
        tout[ch, own_out] = outs[ch][...]

    def share_tokens(ch):
        for slot in (4 * e + c, 4 * d + far, 4 * e + far):
            got(tin.at[ch, slot], tin_sem.at[ch, slot])
            send(tin.at[ch, slot], tin.at[ch, slot], tin_sem.at[ch, slot], sibling)

    def rotate_in_part(ch):
        sib_far = lax.rem(sib + 2, 4)
        for slot in (4 * d + sib, 4 * e + sib, 4 * d + sib_far, 4 * e + sib_far):
            got(tin.at[ch, slot], tin_sem.at[ch, slot])
        mine[ch].wait()
        if ch == 0:
            loads[0].wait()
        for half in (e, d):
            block = flat(tin[ch, pl.ds(4 * half, 4)])
            value = dot(block, basis_in[...]).astype(bf16)
            pin[ch, pl.ds(4 * half, 4)] = value.reshape(4, -1, value.shape[-1])
            if half is e:
                send(pin.at[ch, pl.ds(4 * e, 4)], xr.at[ch], xr_sem.at[ch], other)

    def scatter_rows(ch):
        got(xr.at[ch], xr_sem.at[ch])
        for j in rows + [r]:
            zs[ch, j] = (pin[ch, 4 * d + j].astype(f32) + xr[ch, j].astype(f32)).astype(bf16)
            if j is not r:
                send(zs.at[ch, j], zr.at[ch, r], zr_sem.at[ch, r], (d, j, c))

    def finish_piece(ch):
        total = zs[ch, r].astype(f32)
        for j in rows:
            got(zr.at[ch, j], zr_sem.at[ch, j])
            total = total + zr[ch, j].astype(f32)
        fin[ch, own_out] = total.astype(bf16)
        for peer in [(d, j, c) for j in rows] + [other]:
            send(fin.at[ch, own_out], fin.at[ch, own_out], fin_sem.at[ch, own_out], peer)

    def forward(buf, sem, ch):
        for j in rows:
            slot = 4 * d + j
            got(buf.at[ch, slot], sem.at[ch, slot])
            send(buf.at[ch, slot], buf.at[ch, slot], sem.at[ch, slot], other)

    def arrive(buf, sem, ch):
        for j in range(4):
            got(buf.at[ch, 4 * e + j], sem.at[ch, 4 * e + j])

    near, away = pl.ds(4 * core, 4), pl.ds(4 * (1 - core), 4)

    def rotate_out_part(ch):
        arrive(tout, tout_sem, ch)
        if ch == 0:
            loads[1].wait()
        for part_rows in (away, near):
            value = dot(flat(tout[ch, part_rows]), basis_out[...]).astype(bf16)
            pout[ch, part_rows] = value.reshape(4, -1, value.shape[-1])
            if part_rows is away:
                send(pout.at[ch, away], sr.at[ch], out_sem.at[ch, 0], sibling)

    def add_sibling(ch):
        got(sr.at[ch], out_sem.at[ch, 0])
        ys[ch] = (pout[ch, near].astype(f32) + sr[ch].astype(f32)).astype(bf16)
        send(ys.at[ch], yr.at[ch], out_sem.at[ch, 1], across)

    def add_across(ch):
        got(yr.at[ch], out_sem.at[ch, 1])
        rot[ch, near] = (ys[ch].astype(f32) + yr[ch].astype(f32)).astype(bf16)
        send(rot.at[ch, near], rot.at[ch, near], out_sem.at[ch, 2], sibling)

    share_tokens(0)
    rotate_in_part(0)
    share_tokens(1)
    rotate_in_part(1)
    scatter_rows(0)
    forward(tout, tout_sem, 0)
    scatter_rows(1)
    finish_piece(0)
    forward(tout, tout_sem, 1)
    rotate_out_part(0)
    add_sibling(0)
    finish_piece(1)
    forward(fin, fin_sem, 0)
    add_across(0)
    rotate_out_part(1)
    forward(fin, fin_sem, 1)
    add_sibling(1)

    arrive(fin, fin_sem, 0)
    got(rot.at[0, away], out_sem.at[0, 2])
    loads[2].wait()
    grad = lax.dot_general(
        flat(rot[0]), flat(fin[0]), (((0,), (0,)), ((), ())), preferred_element_type=f32
    )
    precond[...] = grad / (eig[...] + damping)

    add_across(1)
    got(rot.at[1, away], out_sem.at[1, 2])
    mixed = dot(flat(rot[1]), precond[...].astype(bf16))
    arrive(fin, fin_sem, 1)
    product = mixed * flat(fin[1]).astype(f32)
    lanes = product[:, :128]
    for at in range(128, product.shape[1], 128):
        lanes = lanes + product[:, at:at + 128]
    line = jnp.sum(lanes.T, axis=0, keepdims=True)
    kept = line.shape[1] // 2
    part[0] = jnp.broadcast_to(line[:, :kept], part.shape[1:])
    part[1] = jnp.broadcast_to(line[:, kept:], part.shape[1:])

    col_sc[c] = part[...]
    for j in cols:
        send(part, col_sc.at[c], sc_sem.at[c], (d, r, j))
    for j in cols:
        got(col_sc.at[j], sc_sem.at[j])
    row_sc[r] = ((col_sc[0] + col_sc[1]) + col_sc[2]) + col_sc[3]
    for j in rows:
        send(row_sc.at[r], row_sc.at[r], sc_sem.at[4 + r], (d, j, c))
    for j in rows:
        got(row_sc.at[j], sc_sem.at[4 + j])
    dp_sc[0:2] = ((row_sc[0] + row_sc[1]) + row_sc[2]) + row_sc[3]
    send(dp_sc.at[e], dp_sc.at[2], sc_sem.at[8], other)
    got(dp_sc.at[2], sc_sem.at[8])
    scores[...] = dp_sc[d] + dp_sc[2]

    for copy in sends:
        copy.wait_send()


def local_plan(query_out, query_in, out_basis, in_basis, eigvals, train_out, train_in):
    own, wide = query_out.shape
    depth, across = in_basis.shape
    narrow = out_basis.shape[1]
    slots = lax.axis_size("dp") * lax.axis_size("row")
    kept = own * lax.axis_size("row")
    vmem = pl.BlockSpec(memory_space=pltpu.VMEM)
    hbm = pl.BlockSpec(memory_space=pl.ANY)
    dma = pltpu.SemaphoreType.DMA
    precond, scores = pl.pallas_call(
        kernel,
        out_shape=(
            jax.ShapeDtypeStruct(eigvals.shape, f32),
            jax.ShapeDtypeStruct((8, kept), f32),
        ),
        in_specs=[vmem, vmem, hbm, hbm, hbm, vmem, vmem],
        out_specs=(vmem, vmem),
        scratch_shapes=[
            pltpu.VMEM(out_basis.shape, bf16),
            pltpu.VMEM(in_basis.shape, bf16),
            pltpu.VMEM(eigvals.shape, f32),
            pltpu.VMEM((2, slots, own, depth), bf16),
            pltpu.VMEM((2, slots, own, across), bf16),
            pltpu.VMEM((2, 4, own, across), bf16),
            pltpu.VMEM((2, 4, own, across), bf16),
            pltpu.VMEM((2, 4, own, across), bf16),
            pltpu.VMEM((2, slots, own, across), bf16),
            pltpu.VMEM((2, slots, own, wide), bf16),
            pltpu.VMEM((2, slots, own, narrow), bf16),
            pltpu.VMEM((2, 4, own, narrow), bf16),
            pltpu.VMEM((2, 4, own, narrow), bf16),
            pltpu.VMEM((2, 4, own, narrow), bf16),
            pltpu.VMEM((2, slots, own, narrow), bf16),
            pltpu.VMEM((2, 8, kept), f32),
            pltpu.VMEM((4, 2, 8, kept), f32),
            pltpu.VMEM((4, 2, 8, kept), f32),
            pltpu.VMEM((3, 8, kept), f32),
            dma((5,)),
            dma((80,)),
            dma((2, 8)),
            dma((2,)),
            dma((2, 4)),
            dma((2, 8)),
            dma((2, 8)),
            dma((2, 3)),
            dma((9,)),
        ],
        compiler_params=pltpu.CompilerParams(
            collective_id=0, has_side_effects=True, vmem_limit_bytes=50 * 2**20
        ),
        cost_estimate=pl.CostEstimate(flops=4 * 10**9, bytes_accessed=10**7, transcendentals=0),
    )(query_out, query_in, out_basis, in_basis, eigvals, train_out, train_in)
    return (precond, scores[0])


def fits(mesh):
    return dict(mesh.shape) == {"dp": 2, "row": 4, "col": 4}


def solution(mesh):
    in_specs = (
        P(("dp", "row"), "col"),
        P(("dp", "col"), None),
        P("col", ("dp", "row")),
        P(("dp", "row"), "col"),
        P(("dp", "row"), "col"),
        P(("dp", "row"), "col"),
        P(("dp", "col"), None),
    )
    out_specs = (P(("dp", "row"), "col"), P("dp"))
    return jax.shard_map(
        local_plan if fits(mesh) else wide_plan, mesh=mesh, in_specs=in_specs, out_specs=out_specs, check_vma=False
    )
```

```python
import functools

import jax
import jax.numpy as jnp
from jax import lax
from jax.experimental import pallas as pl
from jax.experimental.pallas import tpu as pltpu
from jax.sharding import PartitionSpec as P

damping = 1.0


def rotate_out(tok_rows, basis_panel):
    gathered = lax.all_gather(tok_rows, "row", axis=0, tiled=True)
    partial_sum = jnp.dot(gathered, basis_panel, preferred_element_type=jnp.float32)
    return lax.psum(partial_sum.astype(jnp.bfloat16), "col")


def rotate_in(tok_rows, basis_panel):
    groups = lax.axis_size("dp")
    row_count = lax.axis_size("row")
    sub_width = tok_rows.shape[1] // (groups * row_count)
    split_rows = tok_rows.reshape(tok_rows.shape[0], groups, row_count, sub_width)
    picked = lax.dynamic_index_in_dim(split_rows, lax.axis_index("row"), 2, keepdims=False)
    picked = picked.reshape(tok_rows.shape[0], groups * sub_width)
    gathered = lax.all_gather(picked, "col", axis=0, tiled=True)
    partial_sum = jnp.dot(gathered, basis_panel, preferred_element_type=jnp.float32)
    return lax.psum(partial_sum.astype(jnp.bfloat16), "row")


def wide_plan(query_out, query_in, out_basis, in_basis, eigvals, train_out, train_in):
    panel_out = lax.all_gather(out_basis, "dp", axis=1, tiled=True)
    panel_in = lax.all_gather(in_basis, "dp", axis=0, tiled=True)
    query_rot = rotate_out(query_out, panel_out)
    query_inr = rotate_in(query_in, panel_in)
    partial_grad = lax.dot_general(
        query_rot, query_inr, (((0,), (0,)), ((), ())), preferred_element_type=jnp.float32
    )
    owned = lax.psum_scatter(
        partial_grad.astype(jnp.bfloat16), "dp", scatter_dimension=0, tiled=True
    ).astype(jnp.float32)
    precond = owned / (eigvals + damping)
    shared = precond.astype(jnp.bfloat16)
    train_rot = rotate_out(train_out, panel_out)
    train_inr = rotate_in(train_in, panel_in)
    mixed = jnp.dot(
        train_rot,
        lax.all_gather(shared, "dp", axis=0, tiled=True),
        preferred_element_type=jnp.float32,
    )
    partial_scores = jnp.sum(mixed * train_inr.astype(jnp.float32), axis=1)
    scores = lax.psum(partial_scores, ("row", "col"))
    return (precond, scores)


bf16 = jnp.bfloat16
f32 = jnp.float32


def dot(left, right):
    return jnp.dot(left, right, preferred_element_type=f32)


def flat(block):
    return block.reshape(-1, block.shape[-1])


def kernel(
    q_out, q_in, basis_out_hbm, basis_in_hbm, eig_hbm, t_out, t_in,
    grad, scores,
    shared, basis_out, basis_in, eig, tin, pin, xr, zs, zr, fin, tout, pout, sr, ys, yr, rot,
    part, col_sc, row_sc, dp_sc,
    local_sem, send_sem, tin_sem, xr_sem, zr_sem, fin_sem, tout_sem, out_sem, sc_sem,
):
    d, r, c = lax.axis_index("dp"), lax.axis_index("row"), lax.axis_index("col")
    e = 1 - d
    core = lax.rem(c, 2)
    sib = c + 1 - 2 * core
    far = lax.rem(c + 2, 4)
    sibling, across, other, diagonal = (d, r, sib), (d, r, far), (e, r, c), (e, r, far)
    rows = [lax.rem(r + k, 4) for k in (1, 2, 3)]
    cols = [lax.rem(c + k, 4) for k in (1, 2, 3)]
    own_out, own_in = 4 * d + r, 4 * d + c
    toks, outs = (q_in, t_in), (q_out, t_out)
    width = basis_in.shape[0]

    loads = [
        pltpu.make_async_copy(basis_in_hbm, basis_in, local_sem.at[0]),
        pltpu.make_async_copy(basis_out_hbm, basis_out, local_sem.at[1]),
        pltpu.make_async_copy(eig_hbm, eig, local_sem.at[2]),
    ]
    for load in loads:
        load.start()

    barrier = pltpu.get_barrier_semaphore()
    peers = [(d, r, j) for j in cols] + [(d, j, c) for j in rows] + [other, diagonal]
    for peer in peers:
        pl.semaphore_signal(barrier, inc=1, device_id=peer, device_id_type=pl.DeviceIdType.MESH)
    pl.semaphore_wait(barrier, len(peers))

    sends = []

    def send(src, dst, sem, peer):
        copy = pltpu.make_async_remote_copy(
            src_ref=src, dst_ref=dst, send_sem=send_sem.at[len(sends)], recv_sem=sem,
            device_id=peer, device_id_type=pl.DeviceIdType.MESH,
        )
        copy.start()
        sends.append(copy)

    def got(dst, sem):
        pltpu.make_async_remote_copy(
            src_ref=dst, dst_ref=dst, send_sem=send_sem.at[0], recv_sem=sem,
            device_id=sibling, device_id_type=pl.DeviceIdType.MESH,
        ).wait_recv()

    def columns(ref, group):
        return ref.at[:, pl.ds(pl.multiple_of((group * 4 + r) * width, width), width)]

    mine, held = [], {}
    for ch in range(2):
        for peer in (other, across, diagonal, sibling):
            send(columns(toks[ch], peer[0]), tin.at[ch, own_in], tin_sem.at[ch, own_in], peer)
        keep = pltpu.make_async_copy(columns(toks[ch], d), tin.at[ch, own_in], local_sem.at[3 + ch])
        keep.start()
        mine.append(keep)

    def spread_out(ch):
        for j in rows:
            send(outs[ch], tout.at[ch, own_out], tout_sem.at[ch, own_out], (d, j, c))

        keep = pltpu.make_async_copy(outs[ch], tout.at[ch, own_out], local_sem.at[5 + ch])
        keep.start()
        held[ch] = keep

    def share_tokens(ch):
        for slot in (4 * e + c, 4 * d + far, 4 * e + far):
            got(tin.at[ch, slot], tin_sem.at[ch, slot])
            send(tin.at[ch, slot], tin.at[ch, slot], tin_sem.at[ch, slot], sibling)

    def rotate_in_part(ch):
        sib_far = lax.rem(sib + 2, 4)
        for slot in (4 * d + sib, 4 * e + sib, 4 * d + sib_far, 4 * e + sib_far):
            got(tin.at[ch, slot], tin_sem.at[ch, slot])
        mine[ch].wait()
        if ch == 0:
            loads[0].wait()
        for half in (e, d):
            block = flat(tin[ch, pl.ds(4 * half, 4)])
            value = dot(block, basis_in[...]).astype(bf16)
            pin[ch, pl.ds(4 * half, 4)] = value.reshape(4, -1, value.shape[-1])
            if half is e:
                for j in rows + [r]:
                    send(pin.at[ch, 4 * e + j], xr.at[ch, j], xr_sem.at[ch, j], other)

    def scatter_rows(ch):
        for j in rows + [r]:
            got(xr.at[ch, j], xr_sem.at[ch, j])
            zs[ch, j] = (pin[ch, 4 * d + j].astype(f32) + xr[ch, j].astype(f32)).astype(bf16)
            if j is not r:
                send(zs.at[ch, j], zr.at[ch, r], zr_sem.at[ch, r], (d, j, c))

    def finish_piece(ch):
        total = zs[ch, r].astype(f32)
        for j in rows:
            got(zr.at[ch, j], zr_sem.at[ch, j])
            total = total + zr[ch, j].astype(f32)
        fin[ch, own_out] = total.astype(bf16)
        for peer in [(d, j, c) for j in rows] + [other]:
            send(fin.at[ch, own_out], fin.at[ch, own_out], fin_sem.at[ch, own_out], peer)

    def forward(buf, sem, ch):
        for j in rows:
            slot = 4 * d + j
            got(buf.at[ch, slot], sem.at[ch, slot])
            send(buf.at[ch, slot], buf.at[ch, slot], sem.at[ch, slot], other)

    def arrive(buf, sem, ch):
        for j in range(4):
            got(buf.at[ch, 4 * e + j], sem.at[ch, 4 * e + j])

    near, away = pl.ds(4 * core, 4), pl.ds(4 * (1 - core), 4)

    def rotate_out_part(ch):
        arrive(tout, tout_sem, ch)
        held[ch].wait()
        if ch == 0:
            loads[1].wait()
        for part_rows in (away, near):
            value = dot(flat(tout[ch, part_rows]), basis_out[...]).astype(bf16)
            pout[ch, part_rows] = value.reshape(4, -1, value.shape[-1])
            if part_rows is away:
                send(pout.at[ch, away], sr.at[ch], out_sem.at[ch, 0], sibling)

    def add_sibling(ch):
        got(sr.at[ch], out_sem.at[ch, 0])
        ys[ch] = (pout[ch, near].astype(f32) + sr[ch].astype(f32)).astype(bf16)
        send(ys.at[ch], yr.at[ch], out_sem.at[ch, 1], across)

    def add_across(ch):
        got(yr.at[ch], out_sem.at[ch, 1])
        rot[ch, near] = (ys[ch].astype(f32) + yr[ch].astype(f32)).astype(bf16)
        send(rot.at[ch, near], rot.at[ch, near], out_sem.at[ch, 2], sibling)

    def forward_out(ch):
        send(outs[ch], tout.at[ch, own_out], tout_sem.at[ch, own_out], other)
        forward(tout, tout_sem, ch)

    spread_out(0)
    share_tokens(0)
    rotate_in_part(0)
    share_tokens(1)
    rotate_in_part(1)
    scatter_rows(0)
    forward_out(0)
    scatter_rows(1)
    spread_out(1)
    finish_piece(0)
    rotate_out_part(0)
    finish_piece(1)
    add_sibling(0)
    forward(fin, fin_sem, 0)
    add_across(0)
    forward_out(1)
    forward(fin, fin_sem, 1)
    rotate_out_part(1)
    add_sibling(1)

    arrive(fin, fin_sem, 0)
    got(rot.at[0, away], out_sem.at[0, 2])
    loads[2].wait()
    value = lax.dot_general(
        flat(rot[0]), flat(fin[0]), (((0,), (0,)), ((), ())), preferred_element_type=f32
    )
    grad[...] = value.astype(bf16)
    shared[...] = (value / (eig[...] + damping)).astype(bf16)

    add_across(1)
    got(rot.at[1, away], out_sem.at[1, 2])
    mixed = dot(flat(rot[1]), shared[...])
    arrive(fin, fin_sem, 1)
    product = mixed * flat(fin[1]).astype(f32)
    lanes = product[:, :128]
    for at in range(128, product.shape[1], 128):
        lanes = lanes + product[:, at:at + 128]
    line = jnp.sum(lanes.T, axis=0, keepdims=True)
    kept = line.shape[1] // 2
    part[0] = jnp.broadcast_to(line[:, :kept], part.shape[1:])
    part[1] = jnp.broadcast_to(line[:, kept:], part.shape[1:])

    col_sc[c] = part[...]
    for j in cols:
        send(part, col_sc.at[c], sc_sem.at[c], (d, r, j))
    for j in cols:
        got(col_sc.at[j], sc_sem.at[j])
    row_sc[r] = ((col_sc[0] + col_sc[1]) + col_sc[2]) + col_sc[3]
    for j in rows:
        send(row_sc.at[r], row_sc.at[r], sc_sem.at[4 + r], (d, j, c))
    for j in rows:
        got(row_sc.at[j], sc_sem.at[4 + j])
    dp_sc[0:2] = ((row_sc[0] + row_sc[1]) + row_sc[2]) + row_sc[3]
    send(dp_sc.at[e], dp_sc.at[2], sc_sem.at[8], other)
    got(dp_sc.at[2], sc_sem.at[8])
    scores[...] = dp_sc[d, 0:1] + dp_sc[2, 0:1]

    for copy in sends:
        copy.wait_send()


def local_plan(query_out, query_in, out_basis, in_basis, eigvals, train_out, train_in):
    own, wide = query_out.shape
    depth, across = in_basis.shape
    narrow = out_basis.shape[1]
    slots = lax.axis_size("dp") * lax.axis_size("row")
    kept = own * lax.axis_size("row")
    vmem = pl.BlockSpec(memory_space=pltpu.VMEM)
    hbm = pl.BlockSpec(memory_space=pl.ANY)
    dma = pltpu.SemaphoreType.DMA
    grad, scores = pl.pallas_call(
        kernel,
        out_shape=(
            jax.ShapeDtypeStruct(eigvals.shape, bf16),
            jax.ShapeDtypeStruct((1, kept), f32),
        ),
        in_specs=[hbm] * 7,
        out_specs=(vmem, vmem),
        scratch_shapes=[
            pltpu.VMEM(eigvals.shape, bf16),
            pltpu.VMEM(out_basis.shape, bf16),
            pltpu.VMEM(in_basis.shape, bf16),
            pltpu.VMEM(eigvals.shape, f32),
            pltpu.VMEM((2, slots, own, depth), bf16),
            pltpu.VMEM((2, slots, own, across), bf16),
            pltpu.VMEM((2, 4, own, across), bf16),
            pltpu.VMEM((2, 4, own, across), bf16),
            pltpu.VMEM((2, 4, own, across), bf16),
            pltpu.VMEM((2, slots, own, across), bf16),
            pltpu.VMEM((2, slots, own, wide), bf16),
            pltpu.VMEM((2, slots, own, narrow), bf16),
            pltpu.VMEM((2, 4, own, narrow), bf16),
            pltpu.VMEM((2, 4, own, narrow), bf16),
            pltpu.VMEM((2, 4, own, narrow), bf16),
            pltpu.VMEM((2, slots, own, narrow), bf16),
            pltpu.VMEM((2, 8, kept), f32),
            pltpu.VMEM((4, 2, 8, kept), f32),
            pltpu.VMEM((4, 2, 8, kept), f32),
            pltpu.VMEM((3, 8, kept), f32),
            dma((7,)),
            dma((80,)),
            dma((2, 8)),
            dma((2, 4)),
            dma((2, 4)),
            dma((2, 8)),
            dma((2, 8)),
            dma((2, 3)),
            dma((9,)),
        ],
        compiler_params=pltpu.CompilerParams(
            collective_id=0, has_side_effects=True, vmem_limit_bytes=63 * 2**20
        ),
        cost_estimate=pl.CostEstimate(flops=4 * 10**9, bytes_accessed=10**7, transcendentals=0),
    )(query_out, query_in, out_basis, in_basis, eigvals, train_out, train_in)
    return (grad.astype(f32) / (eigvals + damping), scores.reshape(kept))


def fits(mesh):
    return dict(mesh.shape) == {"dp": 2, "row": 4, "col": 4}


def solution(mesh):
    in_specs = (
        P(("dp", "row"), "col"),
        P(("dp", "col"), None),
        P("col", ("dp", "row")),
        P(("dp", "row"), "col"),
        P(("dp", "row"), "col"),
        P(("dp", "row"), "col"),
        P(("dp", "col"), None),
    )
    out_specs = (P(("dp", "row"), "col"), P("dp"))
    return jax.shard_map(
        local_plan if fits(mesh) else wide_plan, mesh=mesh, in_specs=in_specs, out_specs=out_specs, check_vma=False
    )
```

```python
import functools

import jax
import jax.numpy as jnp
from jax import lax
from jax.experimental import pallas as pl
from jax.experimental.pallas import tpu as pltpu
from jax.sharding import PartitionSpec as P

damping = 1.0


def rotate_out(tok_rows, basis_panel):
    gathered = lax.all_gather(tok_rows, "row", axis=0, tiled=True)
    partial_sum = jnp.dot(gathered, basis_panel, preferred_element_type=jnp.float32)
    return lax.psum(partial_sum.astype(jnp.bfloat16), "col")


def rotate_in(tok_rows, basis_panel):
    groups = lax.axis_size("dp")
    row_count = lax.axis_size("row")
    sub_width = tok_rows.shape[1] // (groups * row_count)
    split_rows = tok_rows.reshape(tok_rows.shape[0], groups, row_count, sub_width)
    picked = lax.dynamic_index_in_dim(split_rows, lax.axis_index("row"), 2, keepdims=False)
    picked = picked.reshape(tok_rows.shape[0], groups * sub_width)
    gathered = lax.all_gather(picked, "col", axis=0, tiled=True)
    partial_sum = jnp.dot(gathered, basis_panel, preferred_element_type=jnp.float32)
    return lax.psum(partial_sum.astype(jnp.bfloat16), "row")


def wide_plan(query_out, query_in, out_basis, in_basis, eigvals, train_out, train_in):
    panel_out = lax.all_gather(out_basis, "dp", axis=1, tiled=True)
    panel_in = lax.all_gather(in_basis, "dp", axis=0, tiled=True)
    query_rot = rotate_out(query_out, panel_out)
    query_inr = rotate_in(query_in, panel_in)
    partial_grad = lax.dot_general(
        query_rot, query_inr, (((0,), (0,)), ((), ())), preferred_element_type=jnp.float32
    )
    owned = lax.psum_scatter(
        partial_grad.astype(jnp.bfloat16), "dp", scatter_dimension=0, tiled=True
    ).astype(jnp.float32)
    precond = owned / (eigvals + damping)
    shared = precond.astype(jnp.bfloat16)
    train_rot = rotate_out(train_out, panel_out)
    train_inr = rotate_in(train_in, panel_in)
    mixed = jnp.dot(
        train_rot,
        lax.all_gather(shared, "dp", axis=0, tiled=True),
        preferred_element_type=jnp.float32,
    )
    partial_scores = jnp.sum(mixed * train_inr.astype(jnp.float32), axis=1)
    scores = lax.psum(partial_scores, ("row", "col"))
    return (precond, scores)


bf16 = jnp.bfloat16
f32 = jnp.float32


def dot(left, right):
    return jnp.dot(left, right, preferred_element_type=f32)


def flat(block):
    return block.reshape(-1, block.shape[-1])


def kernel(
    q_out_hbm, q_in_hbm, basis_out_hbm, basis_in_hbm, eig_hbm, t_out_hbm, t_in_hbm,
    grad, scores,
    q_in, t_in, q_out, t_out, shared, basis_out, basis_in, eig, tin, pin, xr, zs, zr, fin, tout, pout, sr, ys, yr, rot,
    part, col_sc, row_sc, dp_sc,
    local_sem, send_sem, tin_sem, xr_sem, zr_sem, fin_sem, tout_sem, out_sem, sc_sem,
):
    d, r, c = lax.axis_index("dp"), lax.axis_index("row"), lax.axis_index("col")
    e = 1 - d
    core = lax.rem(c, 2)
    sib = c + 1 - 2 * core
    far = lax.rem(c + 2, 4)
    sibling, across, other, diagonal = (d, r, sib), (d, r, far), (e, r, c), (e, r, far)
    rows = [lax.rem(r + k, 4) for k in (1, 2, 3)]
    cols = [lax.rem(c + k, 4) for k in (1, 2, 3)]
    own_out, own_in = 4 * d + r, 4 * d + c
    toks, outs = (q_in, t_in), (q_out, t_out)
    width = basis_in.shape[0]

    loads = [
        pltpu.make_async_copy(basis_in_hbm, basis_in, local_sem.at[0]),
        pltpu.make_async_copy(basis_out_hbm, basis_out, local_sem.at[1]),
        pltpu.make_async_copy(eig_hbm, eig, local_sem.at[2]),
    ]
    tokens = [
        pltpu.make_async_copy(src, dst, local_sem.at[7 + k])
        for k, (src, dst) in enumerate(
            ((q_in_hbm, q_in), (t_in_hbm, t_in), (q_out_hbm, q_out), (t_out_hbm, t_out))
        )
    ]
    for load in tokens + loads:
        load.start()

    barrier = pltpu.get_barrier_semaphore()
    peers = [(d, r, j) for j in cols] + [(d, j, c) for j in rows] + [other, diagonal]
    for peer in peers:
        pl.semaphore_signal(barrier, inc=1, device_id=peer, device_id_type=pl.DeviceIdType.MESH)
    pl.semaphore_wait(barrier, len(peers))

    sends = []

    def send(src, dst, sem, peer):
        copy = pltpu.make_async_remote_copy(
            src_ref=src, dst_ref=dst, send_sem=send_sem.at[len(sends)], recv_sem=sem,
            device_id=peer, device_id_type=pl.DeviceIdType.MESH,
        )
        copy.start()
        sends.append(copy)

    def got(dst, sem):
        pltpu.make_async_remote_copy(
            src_ref=dst, dst_ref=dst, send_sem=send_sem.at[0], recv_sem=sem,
            device_id=sibling, device_id_type=pl.DeviceIdType.MESH,
        ).wait_recv()

    def columns(ref, group):
        return ref.at[:, pl.ds(pl.multiple_of((group * 4 + r) * width, width), width)]

    mine, held = [], {}
    for ch in range(2):
        tokens[ch].wait()
        for peer in (other, across, diagonal, sibling):
            send(columns(toks[ch], peer[0]), tin.at[ch, own_in], tin_sem.at[ch, own_in], peer)
        keep = pltpu.make_async_copy(columns(toks[ch], d), tin.at[ch, own_in], local_sem.at[3 + ch])
        keep.start()
        mine.append(keep)

    def spread_out(ch):
        tokens[2 + ch].wait()
        for j in rows:
            send(outs[ch], tout.at[ch, own_out], tout_sem.at[ch, own_out], (d, j, c))

        keep = pltpu.make_async_copy(outs[ch], tout.at[ch, own_out], local_sem.at[5 + ch])
        keep.start()
        held[ch] = keep

    def share_tokens(ch):
        for slot in (4 * e + c, 4 * d + far, 4 * e + far):
            got(tin.at[ch, slot], tin_sem.at[ch, slot])
            send(tin.at[ch, slot], tin.at[ch, slot], tin_sem.at[ch, slot], sibling)

    def rotate_in_part(ch):
        sib_far = lax.rem(sib + 2, 4)
        for slot in (4 * d + sib, 4 * e + sib, 4 * d + sib_far, 4 * e + sib_far):
            got(tin.at[ch, slot], tin_sem.at[ch, slot])
        mine[ch].wait()
        if ch == 0:
            loads[0].wait()
        for half in (e, d):
            block = flat(tin[ch, pl.ds(4 * half, 4)])
            value = dot(block, basis_in[...]).astype(bf16)
            pin[ch, pl.ds(4 * half, 4)] = value.reshape(4, -1, value.shape[-1])
            if half is e:
                for j in rows + [r]:
                    send(pin.at[ch, 4 * e + j], xr.at[ch, j], xr_sem.at[ch, j], other)

    def scatter_rows(ch):
        for j in rows + [r]:
            got(xr.at[ch, j], xr_sem.at[ch, j])
            zs[ch, j] = (pin[ch, 4 * d + j].astype(f32) + xr[ch, j].astype(f32)).astype(bf16)
            if j is not r:
                send(zs.at[ch, j], zr.at[ch, r], zr_sem.at[ch, r], (d, j, c))

    def finish_piece(ch):
        total = zs[ch, r].astype(f32)
        for j in rows:
            got(zr.at[ch, j], zr_sem.at[ch, j])
            total = total + zr[ch, j].astype(f32)
        fin[ch, own_out] = total.astype(bf16)
        for peer in [(d, j, c) for j in rows] + [other]:
            send(fin.at[ch, own_out], fin.at[ch, own_out], fin_sem.at[ch, own_out], peer)

    def forward(buf, sem, ch):
        for j in rows:
            slot = 4 * d + j
            got(buf.at[ch, slot], sem.at[ch, slot])
            send(buf.at[ch, slot], buf.at[ch, slot], sem.at[ch, slot], other)

    def arrive(buf, sem, ch):
        for j in range(4):
            got(buf.at[ch, 4 * e + j], sem.at[ch, 4 * e + j])

    near, away = pl.ds(4 * core, 4), pl.ds(4 * (1 - core), 4)

    def rotate_out_part(ch):
        arrive(tout, tout_sem, ch)
        held[ch].wait()
        if ch == 0:
            loads[1].wait()
        for part_rows in (away, near):
            value = dot(flat(tout[ch, part_rows]), basis_out[...]).astype(bf16)
            pout[ch, part_rows] = value.reshape(4, -1, value.shape[-1])
            if part_rows is away:
                send(pout.at[ch, away], sr.at[ch], out_sem.at[ch, 0], sibling)

    def add_sibling(ch):
        got(sr.at[ch], out_sem.at[ch, 0])
        ys[ch] = (pout[ch, near].astype(f32) + sr[ch].astype(f32)).astype(bf16)
        send(ys.at[ch], yr.at[ch], out_sem.at[ch, 1], across)

    def add_across(ch):
        got(yr.at[ch], out_sem.at[ch, 1])
        rot[ch, near] = (ys[ch].astype(f32) + yr[ch].astype(f32)).astype(bf16)
        send(rot.at[ch, near], rot.at[ch, near], out_sem.at[ch, 2], sibling)

    def forward_out(ch):
        send(outs[ch], tout.at[ch, own_out], tout_sem.at[ch, own_out], other)
        forward(tout, tout_sem, ch)

    spread_out(0)
    spread_out(1)
    share_tokens(0)
    rotate_in_part(0)
    share_tokens(1)
    rotate_in_part(1)
    scatter_rows(0)
    forward_out(0)
    scatter_rows(1)
    finish_piece(0)
    forward_out(1)
    rotate_out_part(0)
    add_sibling(0)
    finish_piece(1)
    forward(fin, fin_sem, 0)
    add_across(0)
    rotate_out_part(1)
    add_sibling(1)
    forward(fin, fin_sem, 1)

    arrive(fin, fin_sem, 0)
    got(rot.at[0, away], out_sem.at[0, 2])
    loads[2].wait()
    value = lax.dot_general(
        flat(rot[0]), flat(fin[0]), (((0,), (0,)), ((), ())), preferred_element_type=f32
    )
    grad[...] = value.astype(bf16)
    shared[...] = (value / (eig[...] + damping)).astype(bf16)

    add_across(1)
    got(rot.at[1, away], out_sem.at[1, 2])
    mixed = dot(flat(rot[1]), shared[...])
    arrive(fin, fin_sem, 1)
    product = mixed * flat(fin[1]).astype(f32)
    lanes = product[:, :128]
    for at in range(128, product.shape[1], 128):
        lanes = lanes + product[:, at:at + 128]
    line = jnp.sum(lanes.T, axis=0, keepdims=True)
    kept = line.shape[1] // 2
    part[0] = jnp.broadcast_to(line[:, :kept], part.shape[1:])
    part[1] = jnp.broadcast_to(line[:, kept:], part.shape[1:])

    col_sc[c] = part[...]
    for j in cols:
        send(part, col_sc.at[c], sc_sem.at[c], (d, r, j))
    for j in cols:
        got(col_sc.at[j], sc_sem.at[j])
    row_sc[r] = ((col_sc[0] + col_sc[1]) + col_sc[2]) + col_sc[3]
    for j in rows:
        send(row_sc.at[r], row_sc.at[r], sc_sem.at[4 + r], (d, j, c))
    for j in rows:
        got(row_sc.at[j], sc_sem.at[4 + j])
    dp_sc[0:2] = ((row_sc[0] + row_sc[1]) + row_sc[2]) + row_sc[3]
    send(dp_sc.at[e], dp_sc.at[2], sc_sem.at[8], other)
    got(dp_sc.at[2], sc_sem.at[8])
    scores[...] = dp_sc[d, 0:1] + dp_sc[2, 0:1]

    for copy in sends:
        copy.wait_send()


def local_plan(query_out, query_in, out_basis, in_basis, eigvals, train_out, train_in):
    own, wide = query_out.shape
    depth, across = in_basis.shape
    narrow = out_basis.shape[1]
    slots = lax.axis_size("dp") * lax.axis_size("row")
    kept = own * lax.axis_size("row")
    vmem = pl.BlockSpec(memory_space=pltpu.VMEM)
    hbm = pl.BlockSpec(memory_space=pl.ANY)
    dma = pltpu.SemaphoreType.DMA
    grad, scores = pl.pallas_call(
        kernel,
        out_shape=(
            jax.ShapeDtypeStruct(eigvals.shape, bf16),
            jax.ShapeDtypeStruct((1, kept), f32),
        ),
        in_specs=[hbm] * 7,
        out_specs=(vmem, vmem),
        scratch_shapes=[
            pltpu.VMEM(query_in.shape, bf16),
            pltpu.VMEM(query_in.shape, bf16),
            pltpu.VMEM(query_out.shape, bf16),
            pltpu.VMEM(query_out.shape, bf16),
            pltpu.VMEM(eigvals.shape, bf16),
            pltpu.VMEM(out_basis.shape, bf16),
            pltpu.VMEM(in_basis.shape, bf16),
            pltpu.VMEM(eigvals.shape, f32),
            pltpu.VMEM((2, slots, own, depth), bf16),
            pltpu.VMEM((2, slots, own, across), bf16),
            pltpu.VMEM((2, 4, own, across), bf16),
            pltpu.VMEM((2, 4, own, across), bf16),
            pltpu.VMEM((2, 4, own, across), bf16),
            pltpu.VMEM((2, slots, own, across), bf16),
            pltpu.VMEM((2, slots, own, wide), bf16),
            pltpu.VMEM((2, slots, own, narrow), bf16),
            pltpu.VMEM((2, 4, own, narrow), bf16),
            pltpu.VMEM((2, 4, own, narrow), bf16),
            pltpu.VMEM((2, 4, own, narrow), bf16),
            pltpu.VMEM((2, slots, own, narrow), bf16),
            pltpu.VMEM((2, 8, kept), f32),
            pltpu.VMEM((4, 2, 8, kept), f32),
            pltpu.VMEM((4, 2, 8, kept), f32),
            pltpu.VMEM((3, 8, kept), f32),
            dma((11,)),
            dma((80,)),
            dma((2, 8)),
            dma((2, 4)),
            dma((2, 4)),
            dma((2, 8)),
            dma((2, 8)),
            dma((2, 3)),
            dma((9,)),
        ],
        compiler_params=pltpu.CompilerParams(
            collective_id=0, has_side_effects=True, vmem_limit_bytes=63 * 2**20
        ),
        cost_estimate=pl.CostEstimate(flops=4 * 10**9, bytes_accessed=10**7, transcendentals=0),
    )(query_out, query_in, out_basis, in_basis, eigvals, train_out, train_in)
    return (grad.astype(f32) / (eigvals + damping), scores.reshape(kept))


def fits(mesh):
    return dict(mesh.shape) == {"dp": 2, "row": 4, "col": 4}


def solution(mesh):
    in_specs = (
        P(("dp", "row"), "col"),
        P(("dp", "col"), None),
        P("col", ("dp", "row")),
        P(("dp", "row"), "col"),
        P(("dp", "row"), "col"),
        P(("dp", "row"), "col"),
        P(("dp", "col"), None),
    )
    out_specs = (P(("dp", "row"), "col"), P("dp"))
    return jax.shard_map(
        local_plan if fits(mesh) else wide_plan, mesh=mesh, in_specs=in_specs, out_specs=out_specs, check_vma=False
    )
```

```python
import functools

import jax
import jax.numpy as jnp
from jax import lax
from jax.experimental import pallas as pl
from jax.experimental.pallas import tpu as pltpu
from jax.sharding import PartitionSpec as P

damping = 1.0


def rotate_out(tok_rows, basis_panel):
    gathered = lax.all_gather(tok_rows, "row", axis=0, tiled=True)
    partial_sum = jnp.dot(gathered, basis_panel, preferred_element_type=jnp.float32)
    return lax.psum(partial_sum.astype(jnp.bfloat16), "col")


def rotate_in(tok_rows, basis_panel):
    groups = lax.axis_size("dp")
    row_count = lax.axis_size("row")
    sub_width = tok_rows.shape[1] // (groups * row_count)
    split_rows = tok_rows.reshape(tok_rows.shape[0], groups, row_count, sub_width)
    picked = lax.dynamic_index_in_dim(split_rows, lax.axis_index("row"), 2, keepdims=False)
    picked = picked.reshape(tok_rows.shape[0], groups * sub_width)
    gathered = lax.all_gather(picked, "col", axis=0, tiled=True)
    partial_sum = jnp.dot(gathered, basis_panel, preferred_element_type=jnp.float32)
    return lax.psum(partial_sum.astype(jnp.bfloat16), "row")


def wide_plan(query_out, query_in, out_basis, in_basis, eigvals, train_out, train_in):
    panel_out = lax.all_gather(out_basis, "dp", axis=1, tiled=True)
    panel_in = lax.all_gather(in_basis, "dp", axis=0, tiled=True)
    query_rot = rotate_out(query_out, panel_out)
    query_inr = rotate_in(query_in, panel_in)
    partial_grad = lax.dot_general(
        query_rot, query_inr, (((0,), (0,)), ((), ())), preferred_element_type=jnp.float32
    )
    owned = lax.psum_scatter(
        partial_grad.astype(jnp.bfloat16), "dp", scatter_dimension=0, tiled=True
    ).astype(jnp.float32)
    precond = owned / (eigvals + damping)
    shared = precond.astype(jnp.bfloat16)
    train_rot = rotate_out(train_out, panel_out)
    train_inr = rotate_in(train_in, panel_in)
    mixed = jnp.dot(
        train_rot,
        lax.all_gather(shared, "dp", axis=0, tiled=True),
        preferred_element_type=jnp.float32,
    )
    partial_scores = jnp.sum(mixed * train_inr.astype(jnp.float32), axis=1)
    scores = lax.psum(partial_scores, ("row", "col"))
    return (precond, scores)


bf16 = jnp.bfloat16
f32 = jnp.float32


def dot(left, right):
    return jnp.dot(left, right, preferred_element_type=f32)


def flat(block):
    return block.reshape(-1, block.shape[-1])


def kernel(
    q_out_hbm, q_in_hbm, basis_out_hbm, basis_in_hbm, eig_hbm, t_out_hbm, t_in_hbm,
    grad, scores,
    q_in, t_in, q_out, t_out, shared, basis_out, basis_in, eig, tin, pin, xr, zs, zr, fin, tout, pout, sr, ys, yr, rot,
    part, col_sc, row_sc, dp_sc,
    local_sem, send_sem, tin_sem, xr_sem, zr_sem, fin_sem, tout_sem, out_sem, sc_sem,
):
    d, r, c = lax.axis_index("dp"), lax.axis_index("row"), lax.axis_index("col")
    e = 1 - d
    core = lax.rem(c, 2)
    sib = c + 1 - 2 * core
    far = lax.rem(c + 2, 4)
    sibling, across, other = (d, r, sib), (d, r, far), (e, r, c)
    rows = [lax.rem(r + k, 4) for k in (1, 2, 3)]
    cols = [lax.rem(c + k, 4) for k in (1, 2, 3)]
    own_out, own_in, kept_row = 4 * d + r, 4 * d + c, 4 * e + r
    toks, outs = (q_in, t_in), (q_out, t_out)
    width = basis_in.shape[0]

    loads = [
        pltpu.make_async_copy(basis_in_hbm, basis_in, local_sem.at[0]),
        pltpu.make_async_copy(basis_out_hbm, basis_out, local_sem.at[1]),
        pltpu.make_async_copy(eig_hbm, eig, local_sem.at[2]),
    ]
    tokens = [
        pltpu.make_async_copy(src, dst, local_sem.at[7 + k])
        for k, (src, dst) in enumerate(
            ((q_in_hbm, q_in), (t_in_hbm, t_in), (q_out_hbm, q_out), (t_out_hbm, t_out))
        )
    ]
    for load in tokens + loads:
        load.start()

    barrier = pltpu.get_barrier_semaphore()
    peers = [(d, r, j) for j in cols] + [(d, j, c) for j in rows] + [other]
    for peer in peers:
        pl.semaphore_signal(barrier, inc=1, device_id=peer, device_id_type=pl.DeviceIdType.MESH)
    pl.semaphore_wait(barrier, len(peers))

    sends = []

    def send(src, dst, sem, peer):
        copy = pltpu.make_async_remote_copy(
            src_ref=src, dst_ref=dst, send_sem=send_sem.at[len(sends)], recv_sem=sem,
            device_id=peer, device_id_type=pl.DeviceIdType.MESH,
        )
        copy.start()
        sends.append(copy)

    def got(dst, sem):
        pltpu.make_async_remote_copy(
            src_ref=dst, dst_ref=dst, send_sem=send_sem.at[0], recv_sem=sem,
            device_id=sibling, device_id_type=pl.DeviceIdType.MESH,
        ).wait_recv()

    def columns(ref, group):
        return ref.at[:, pl.ds(pl.multiple_of((group * 4 + r) * width, width), width)]

    mine, held = [], {}
    for ch in range(2):
        tokens[ch].wait()
        for peer in (other, across, sibling):
            send(columns(toks[ch], peer[0]), tin.at[ch, own_in], tin_sem.at[ch, own_in], peer)
        keep = pltpu.make_async_copy(columns(toks[ch], d), tin.at[ch, own_in], local_sem.at[3 + ch])
        keep.start()
        mine.append(keep)

    def spread_out(ch):
        tokens[2 + ch].wait()
        for j in rows:
            send(outs[ch], tout.at[ch, own_out], tout_sem.at[ch, own_out], (d, j, c))

        keep = pltpu.make_async_copy(outs[ch], tout.at[ch, own_out], local_sem.at[5 + ch])
        keep.start()
        held[ch] = keep

    sib_far = lax.rem(sib + 2, 4)

    def pass_tokens(ch, slot, targets):
        got(tin.at[ch, slot], tin_sem.at[ch, slot])
        for peer in targets:
            send(tin.at[ch, slot], tin.at[ch, slot], tin_sem.at[ch, slot], peer)

    def rotate_half(ch, half):
        for slot in (4 * half + sib, 4 * half + sib_far):
            got(tin.at[ch, slot], tin_sem.at[ch, slot])
        value = dot(flat(tin[ch, pl.ds(4 * half, 4)]), basis_in[...]).astype(bf16)
        pin[ch, pl.ds(4 * half, 4)] = value.reshape(4, -1, value.shape[-1])

    def rotate_own(ch):
        mine[ch].wait()
        if ch == 0:
            loads[0].wait()
        rotate_half(ch, d)
        for j in rows + [r]:
            send(pin.at[ch, 4 * d + j], xr.at[ch, j], xr_sem.at[ch, j], other)

    def scatter_rows(ch):
        for j in rows + [r]:
            got(xr.at[ch, j], xr_sem.at[ch, j])
            zs[ch, j] = (pin[ch, 4 * e + j].astype(f32) + xr[ch, j].astype(f32)).astype(bf16)
            if j is not r:
                send(zs.at[ch, j], zr.at[ch, r], zr_sem.at[ch, r], (d, j, c))

    def finish_piece(ch):
        total = zs[ch, r].astype(f32)
        for j in rows:
            got(zr.at[ch, j], zr_sem.at[ch, j])
            total = total + zr[ch, j].astype(f32)
        fin[ch, kept_row] = total.astype(bf16)
        for peer in [(d, j, c) for j in rows] + [other]:
            send(fin.at[ch, kept_row], fin.at[ch, kept_row], fin_sem.at[ch, kept_row], peer)

    def forward(buf, sem, ch, half):
        for j in rows:
            slot = 4 * half + j
            got(buf.at[ch, slot], sem.at[ch, slot])
            send(buf.at[ch, slot], buf.at[ch, slot], sem.at[ch, slot], other)

    def arrive(buf, sem, ch, half):
        for j in range(4):
            got(buf.at[ch, 4 * half + j], sem.at[ch, 4 * half + j])

    near, away = pl.ds(4 * core, 4), pl.ds(4 * (1 - core), 4)

    def rotate_out_part(ch):
        arrive(tout, tout_sem, ch, e)
        held[ch].wait()
        if ch == 0:
            loads[1].wait()
        for part_rows in (away, near):
            value = dot(flat(tout[ch, part_rows]), basis_out[...]).astype(bf16)
            pout[ch, part_rows] = value.reshape(4, -1, value.shape[-1])
            if part_rows is away:
                send(pout.at[ch, away], sr.at[ch], out_sem.at[ch, 0], sibling)

    def add_sibling(ch):
        got(sr.at[ch], out_sem.at[ch, 0])
        ys[ch] = (pout[ch, near].astype(f32) + sr[ch].astype(f32)).astype(bf16)
        send(ys.at[ch], yr.at[ch], out_sem.at[ch, 1], across)

    def add_across(ch):
        got(yr.at[ch], out_sem.at[ch, 1])
        rot[ch, near] = (ys[ch].astype(f32) + yr[ch].astype(f32)).astype(bf16)
        send(rot.at[ch, near], rot.at[ch, near], out_sem.at[ch, 2], sibling)

    def send_own_out(ch):
        send(outs[ch], tout.at[ch, own_out], tout_sem.at[ch, own_out], other)

    spread_out(0)
    send_own_out(0)
    spread_out(1)
    pass_tokens(0, 4 * d + far, [sibling])
    rotate_own(0)
    pass_tokens(1, 4 * d + far, [sibling])
    rotate_own(1)
    for ch in range(2):
        pass_tokens(ch, 4 * e + c, [across, sibling])
    for ch in range(2):
        pass_tokens(ch, 4 * e + far, [sibling])
    for ch in range(2):
        rotate_half(ch, e)
    scatter_rows(0)
    forward(tout, tout_sem, 0, d)
    scatter_rows(1)
    finish_piece(0)
    send_own_out(1)
    forward(tout, tout_sem, 1, d)
    rotate_out_part(0)
    add_sibling(0)
    finish_piece(1)
    forward(fin, fin_sem, 0, e)
    add_across(0)
    rotate_out_part(1)
    add_sibling(1)
    forward(fin, fin_sem, 1, e)

    arrive(fin, fin_sem, 0, d)
    got(rot.at[0, away], out_sem.at[0, 2])
    loads[2].wait()
    value = lax.dot_general(
        flat(rot[0]), flat(fin[0]), (((0,), (0,)), ((), ())), preferred_element_type=f32
    )
    grad[...] = value.astype(bf16)
    shared[...] = (value / (eig[...] + damping)).astype(bf16)

    add_across(1)
    got(rot.at[1, away], out_sem.at[1, 2])
    mixed = dot(flat(rot[1]), shared[...])
    arrive(fin, fin_sem, 1, d)
    product = mixed * flat(fin[1]).astype(f32)
    lanes = product[:, :128]
    for at in range(128, product.shape[1], 128):
        lanes = lanes + product[:, at:at + 128]
    line = jnp.sum(lanes.T, axis=0, keepdims=True)
    kept = line.shape[1] // 2
    part[0] = jnp.broadcast_to(line[:, :kept], part.shape[1:])
    part[1] = jnp.broadcast_to(line[:, kept:], part.shape[1:])

    col_sc[c] = part[...]
    for j in cols:
        send(part, col_sc.at[c], sc_sem.at[c], (d, r, j))
    for j in cols:
        got(col_sc.at[j], sc_sem.at[j])
    row_sc[r] = ((col_sc[0] + col_sc[1]) + col_sc[2]) + col_sc[3]
    for j in rows:
        send(row_sc.at[r], row_sc.at[r], sc_sem.at[4 + r], (d, j, c))
    for j in rows:
        got(row_sc.at[j], sc_sem.at[4 + j])
    dp_sc[0:2] = ((row_sc[0] + row_sc[1]) + row_sc[2]) + row_sc[3]
    send(dp_sc.at[e], dp_sc.at[2], sc_sem.at[8], other)
    got(dp_sc.at[2], sc_sem.at[8])
    scores[...] = dp_sc[d, 0:1] + dp_sc[2, 0:1]

    for copy in sends:
        copy.wait_send()


def local_plan(query_out, query_in, out_basis, in_basis, eigvals, train_out, train_in):
    own, wide = query_out.shape
    depth, across = in_basis.shape
    narrow = out_basis.shape[1]
    slots = lax.axis_size("dp") * lax.axis_size("row")
    kept = own * lax.axis_size("row")
    vmem = pl.BlockSpec(memory_space=pltpu.VMEM)
    hbm = pl.BlockSpec(memory_space=pl.ANY)
    dma = pltpu.SemaphoreType.DMA
    grad, scores = pl.pallas_call(
        kernel,
        out_shape=(
            jax.ShapeDtypeStruct(eigvals.shape, bf16),
            jax.ShapeDtypeStruct((1, kept), f32),
        ),
        in_specs=[hbm] * 7,
        out_specs=(vmem, vmem),
        scratch_shapes=[
            pltpu.VMEM(query_in.shape, bf16),
            pltpu.VMEM(query_in.shape, bf16),
            pltpu.VMEM(query_out.shape, bf16),
            pltpu.VMEM(query_out.shape, bf16),
            pltpu.VMEM(eigvals.shape, bf16),
            pltpu.VMEM(out_basis.shape, bf16),
            pltpu.VMEM(in_basis.shape, bf16),
            pltpu.VMEM(eigvals.shape, f32),
            pltpu.VMEM((2, slots, own, depth), bf16),
            pltpu.VMEM((2, slots, own, across), bf16),
            pltpu.VMEM((2, 4, own, across), bf16),
            pltpu.VMEM((2, 4, own, across), bf16),
            pltpu.VMEM((2, 4, own, across), bf16),
            pltpu.VMEM((2, slots, own, across), bf16),
            pltpu.VMEM((2, slots, own, wide), bf16),
            pltpu.VMEM((2, slots, own, narrow), bf16),
            pltpu.VMEM((2, 4, own, narrow), bf16),
            pltpu.VMEM((2, 4, own, narrow), bf16),
            pltpu.VMEM((2, 4, own, narrow), bf16),
            pltpu.VMEM((2, slots, own, narrow), bf16),
            pltpu.VMEM((2, 8, kept), f32),
            pltpu.VMEM((4, 2, 8, kept), f32),
            pltpu.VMEM((4, 2, 8, kept), f32),
            pltpu.VMEM((3, 8, kept), f32),
            dma((11,)),
            dma((80,)),
            dma((2, 8)),
            dma((2, 4)),
            dma((2, 4)),
            dma((2, 8)),
            dma((2, 8)),
            dma((2, 3)),
            dma((9,)),
        ],
        compiler_params=pltpu.CompilerParams(
            collective_id=0, has_side_effects=True, vmem_limit_bytes=63 * 2**20
        ),
        cost_estimate=pl.CostEstimate(flops=4 * 10**9, bytes_accessed=10**7, transcendentals=0),
    )(query_out, query_in, out_basis, in_basis, eigvals, train_out, train_in)
    return (grad.astype(f32) / (eigvals + damping), scores.reshape(kept))


def fits(mesh):
    return dict(mesh.shape) == {"dp": 2, "row": 4, "col": 4}


def solution(mesh):
    in_specs = (
        P(("dp", "row"), "col"),
        P(("dp", "col"), None),
        P("col", ("dp", "row")),
        P(("dp", "row"), "col"),
        P(("dp", "row"), "col"),
        P(("dp", "row"), "col"),
        P(("dp", "col"), None),
    )
    out_specs = (P(("dp", "row"), "col"), P("dp"))
    return jax.shard_map(
        local_plan if fits(mesh) else wide_plan, mesh=mesh, in_specs=in_specs, out_specs=out_specs, check_vma=False
    )
```

```python
import functools

import jax
import jax.numpy as jnp
from jax import lax
from jax.experimental import pallas as pl
from jax.experimental.pallas import tpu as pltpu
from jax.sharding import PartitionSpec as P

damping = 1.0


def rotate_out(tok_rows, basis_panel):
    gathered = lax.all_gather(tok_rows, "row", axis=0, tiled=True)
    partial_sum = jnp.dot(gathered, basis_panel, preferred_element_type=jnp.float32)
    return lax.psum(partial_sum.astype(jnp.bfloat16), "col")


def rotate_in(tok_rows, basis_panel):
    groups = lax.axis_size("dp")
    row_count = lax.axis_size("row")
    sub_width = tok_rows.shape[1] // (groups * row_count)
    split_rows = tok_rows.reshape(tok_rows.shape[0], groups, row_count, sub_width)
    picked = lax.dynamic_index_in_dim(split_rows, lax.axis_index("row"), 2, keepdims=False)
    picked = picked.reshape(tok_rows.shape[0], groups * sub_width)
    gathered = lax.all_gather(picked, "col", axis=0, tiled=True)
    partial_sum = jnp.dot(gathered, basis_panel, preferred_element_type=jnp.float32)
    return lax.psum(partial_sum.astype(jnp.bfloat16), "row")


def wide_plan(query_out, query_in, out_basis, in_basis, eigvals, train_out, train_in):
    panel_out = lax.all_gather(out_basis, "dp", axis=1, tiled=True)
    panel_in = lax.all_gather(in_basis, "dp", axis=0, tiled=True)
    query_rot = rotate_out(query_out, panel_out)
    query_inr = rotate_in(query_in, panel_in)
    partial_grad = lax.dot_general(
        query_rot, query_inr, (((0,), (0,)), ((), ())), preferred_element_type=jnp.float32
    )
    owned = lax.psum_scatter(
        partial_grad.astype(jnp.bfloat16), "dp", scatter_dimension=0, tiled=True
    ).astype(jnp.float32)
    precond = owned / (eigvals + damping)
    shared = precond.astype(jnp.bfloat16)
    train_rot = rotate_out(train_out, panel_out)
    train_inr = rotate_in(train_in, panel_in)
    mixed = jnp.dot(
        train_rot,
        lax.all_gather(shared, "dp", axis=0, tiled=True),
        preferred_element_type=jnp.float32,
    )
    partial_scores = jnp.sum(mixed * train_inr.astype(jnp.float32), axis=1)
    scores = lax.psum(partial_scores, ("row", "col"))
    return (precond, scores)


bf16 = jnp.bfloat16
f32 = jnp.float32


def dot(left, right):
    return jnp.dot(left, right, preferred_element_type=f32)


def flat(block):
    return block.reshape(-1, block.shape[-1])


def kernel(
    q_out_hbm, q_in_hbm, basis_out_hbm, basis_in_hbm, eig_hbm, t_out_hbm, t_in_hbm,
    grad, scores,
    q_in, t_in, q_out, t_out, shared, basis_out, basis_in, eig, tin, pin, xr, zs, zr, fin, tout, pout, sr, ys, yr, rot,
    part, col_sc, row_sc, dp_sc,
    local_sem, send_sem, tin_sem, xr_sem, zr_sem, fin_sem, tout_sem, out_sem, sc_sem,
):
    d, r, c = lax.axis_index("dp"), lax.axis_index("row"), lax.axis_index("col")
    e = 1 - d
    core = lax.rem(c, 2)
    sib = c + 1 - 2 * core
    far = lax.rem(c + 2, 4)
    sibling, across, other = (d, r, sib), (d, r, far), (e, r, c)
    rows = [lax.rem(r + k, 4) for k in (1, 2, 3)]
    ring = [lax.rem(r + k, 4) for k in (3, 2, 1, 0)]
    onward = (d, lax.rem(r + 1, 4), c)
    cols = [lax.rem(c + k, 4) for k in (1, 2, 3)]
    own_out, own_in, kept_row = 4 * d + r, 4 * d + c, 4 * e + r
    toks, outs = (q_in, t_in), (q_out, t_out)
    width = basis_in.shape[0]

    loads = [
        pltpu.make_async_copy(basis_in_hbm, basis_in, local_sem.at[0]),
        pltpu.make_async_copy(basis_out_hbm, basis_out, local_sem.at[1]),
        pltpu.make_async_copy(eig_hbm, eig, local_sem.at[2]),
    ]
    tokens = [
        pltpu.make_async_copy(src, dst, local_sem.at[7 + k])
        for k, (src, dst) in enumerate(
            ((q_in_hbm, q_in), (t_in_hbm, t_in), (q_out_hbm, q_out), (t_out_hbm, t_out))
        )
    ]
    for load in tokens + loads:
        load.start()

    barrier = pltpu.get_barrier_semaphore()
    peers = [(d, r, j) for j in cols] + [(d, j, c) for j in rows] + [other]
    for peer in peers:
        pl.semaphore_signal(barrier, inc=1, device_id=peer, device_id_type=pl.DeviceIdType.MESH)
    pl.semaphore_wait(barrier, len(peers))

    sends = []

    def send(src, dst, sem, peer):
        copy = pltpu.make_async_remote_copy(
            src_ref=src, dst_ref=dst, send_sem=send_sem.at[len(sends)], recv_sem=sem,
            device_id=peer, device_id_type=pl.DeviceIdType.MESH,
        )
        copy.start()
        sends.append(copy)

    def got(dst, sem):
        pltpu.make_async_remote_copy(
            src_ref=dst, dst_ref=dst, send_sem=send_sem.at[0], recv_sem=sem,
            device_id=sibling, device_id_type=pl.DeviceIdType.MESH,
        ).wait_recv()

    def columns(ref, group):
        return ref.at[:, pl.ds(pl.multiple_of((group * 4 + r) * width, width), width)]

    mine, held = [], {}
    for ch in range(2):
        tokens[ch].wait()
        for peer in (other, across, sibling):
            send(columns(toks[ch], peer[0]), tin.at[ch, own_in], tin_sem.at[ch, own_in], peer)
        keep = pltpu.make_async_copy(columns(toks[ch], d), tin.at[ch, own_in], local_sem.at[3 + ch])
        keep.start()
        mine.append(keep)

    def spread_out(ch):
        tokens[2 + ch].wait()
        for j in rows:
            send(outs[ch], tout.at[ch, own_out], tout_sem.at[ch, own_out], (d, j, c))

        keep = pltpu.make_async_copy(outs[ch], tout.at[ch, own_out], local_sem.at[5 + ch])
        keep.start()
        held[ch] = keep

    sib_far = lax.rem(sib + 2, 4)

    def pass_tokens(ch, slot, targets):
        got(tin.at[ch, slot], tin_sem.at[ch, slot])
        for peer in targets:
            send(tin.at[ch, slot], tin.at[ch, slot], tin_sem.at[ch, slot], peer)

    def rotate_half(ch, half):
        for slot in (4 * half + sib, 4 * half + sib_far):
            got(tin.at[ch, slot], tin_sem.at[ch, slot])
        value = dot(flat(tin[ch, pl.ds(4 * half, 4)]), basis_in[...]).astype(bf16)
        pin[ch, pl.ds(4 * half, 4)] = value.reshape(4, -1, value.shape[-1])

    def rotate_own(ch):
        mine[ch].wait()
        if ch == 0:
            loads[0].wait()
        rotate_half(ch, d)
        for j in ring:
            send(pin.at[ch, 4 * d + j], xr.at[ch, j], xr_sem.at[ch, j], other)

    def scatter_step(ch, k):
        j = ring[k]
        got(xr.at[ch, j], xr_sem.at[ch, j])
        total = pin[ch, 4 * e + j].astype(f32) + xr[ch, j].astype(f32)
        if k > 0:
            got(zr.at[ch, j], zr_sem.at[ch, j])
            total = total + zr[ch, j].astype(f32)
        if k < 3:
            zs[ch, j] = total.astype(bf16)
            send(zs.at[ch, j], zr.at[ch, j], zr_sem.at[ch, j], onward)
        else:
            fin[ch, kept_row] = total.astype(bf16)
            for peer in (onward, other):
                send(fin.at[ch, kept_row], fin.at[ch, kept_row], fin_sem.at[ch, kept_row], peer)

    def gather_step(ch, k):
        slot = 4 * e + ring[k]
        got(fin.at[ch, slot], fin_sem.at[ch, slot])
        for peer in (onward, other) if k < 2 else (other,):
            send(fin.at[ch, slot], fin.at[ch, slot], fin_sem.at[ch, slot], peer)

    def forward(buf, sem, ch, half):
        for j in rows:
            slot = 4 * half + j
            got(buf.at[ch, slot], sem.at[ch, slot])
            send(buf.at[ch, slot], buf.at[ch, slot], sem.at[ch, slot], other)

    def arrive(buf, sem, ch, half):
        for j in range(4):
            got(buf.at[ch, 4 * half + j], sem.at[ch, 4 * half + j])

    near, away = pl.ds(4 * core, 4), pl.ds(4 * (1 - core), 4)

    def rotate_out_part(ch):
        arrive(tout, tout_sem, ch, e)
        held[ch].wait()
        if ch == 0:
            loads[1].wait()
        for part_rows in (away, near):
            value = dot(flat(tout[ch, part_rows]), basis_out[...]).astype(bf16)
            pout[ch, part_rows] = value.reshape(4, -1, value.shape[-1])
            if part_rows is away:
                send(pout.at[ch, away], sr.at[ch], out_sem.at[ch, 0], sibling)

    def add_sibling(ch):
        got(sr.at[ch], out_sem.at[ch, 0])
        ys[ch] = (pout[ch, near].astype(f32) + sr[ch].astype(f32)).astype(bf16)
        send(ys.at[ch], yr.at[ch], out_sem.at[ch, 1], across)

    def add_across(ch):
        got(yr.at[ch], out_sem.at[ch, 1])
        rot[ch, near] = (ys[ch].astype(f32) + yr[ch].astype(f32)).astype(bf16)
        send(rot.at[ch, near], rot.at[ch, near], out_sem.at[ch, 2], sibling)

    def send_own_out(ch):
        send(outs[ch], tout.at[ch, own_out], tout_sem.at[ch, own_out], other)

    spread_out(0)
    send_own_out(0)
    spread_out(1)
    pass_tokens(0, 4 * d + far, [sibling])
    rotate_own(0)
    pass_tokens(1, 4 * d + far, [sibling])
    rotate_own(1)
    for ch in range(2):
        pass_tokens(ch, 4 * e + c, [across, sibling])
    for ch in range(2):
        pass_tokens(ch, 4 * e + far, [sibling])
    for ch in range(2):
        rotate_half(ch, e)
    for k in range(4):
        scatter_step(0, k)
    forward(tout, tout_sem, 0, d)
    for k in range(3):
        scatter_step(1, k)
        gather_step(0, k)
    scatter_step(1, 3)
    send_own_out(1)
    forward(tout, tout_sem, 1, d)
    rotate_out_part(0)
    add_sibling(0)
    gather_step(1, 0)
    add_across(0)
    gather_step(1, 1)
    rotate_out_part(1)
    add_sibling(1)
    gather_step(1, 2)

    arrive(fin, fin_sem, 0, d)
    got(rot.at[0, away], out_sem.at[0, 2])
    loads[2].wait()
    value = lax.dot_general(
        flat(rot[0]), flat(fin[0]), (((0,), (0,)), ((), ())), preferred_element_type=f32
    )
    grad[...] = value.astype(bf16)
    shared[...] = (value / (eig[...] + damping)).astype(bf16)

    add_across(1)
    got(rot.at[1, away], out_sem.at[1, 2])
    mixed = dot(flat(rot[1]), shared[...])
    arrive(fin, fin_sem, 1, d)
    product = mixed * flat(fin[1]).astype(f32)
    lanes = product[:, :128]
    for at in range(128, product.shape[1], 128):
        lanes = lanes + product[:, at:at + 128]
    line = jnp.sum(lanes.T, axis=0, keepdims=True)
    kept = line.shape[1] // 2
    part[0] = jnp.broadcast_to(line[:, :kept], part.shape[1:])
    part[1] = jnp.broadcast_to(line[:, kept:], part.shape[1:])

    col_sc[c] = part[...]
    for j in cols:
        send(part, col_sc.at[c], sc_sem.at[c], (d, r, j))
    for j in cols:
        got(col_sc.at[j], sc_sem.at[j])
    row_sc[r] = ((col_sc[0] + col_sc[1]) + col_sc[2]) + col_sc[3]
    for j in rows:
        send(row_sc.at[r], row_sc.at[r], sc_sem.at[4 + r], (d, j, c))
    for j in rows:
        got(row_sc.at[j], sc_sem.at[4 + j])
    dp_sc[0:2] = ((row_sc[0] + row_sc[1]) + row_sc[2]) + row_sc[3]
    send(dp_sc.at[e], dp_sc.at[2], sc_sem.at[8], other)
    got(dp_sc.at[2], sc_sem.at[8])
    scores[...] = dp_sc[d, 0:1] + dp_sc[2, 0:1]

    for copy in sends:
        copy.wait_send()


def local_plan(query_out, query_in, out_basis, in_basis, eigvals, train_out, train_in):
    own, wide = query_out.shape
    depth, across = in_basis.shape
    narrow = out_basis.shape[1]
    slots = lax.axis_size("dp") * lax.axis_size("row")
    kept = own * lax.axis_size("row")
    vmem = pl.BlockSpec(memory_space=pltpu.VMEM)
    hbm = pl.BlockSpec(memory_space=pl.ANY)
    dma = pltpu.SemaphoreType.DMA
    grad, scores = pl.pallas_call(
        kernel,
        out_shape=(
            jax.ShapeDtypeStruct(eigvals.shape, bf16),
            jax.ShapeDtypeStruct((1, kept), f32),
        ),
        in_specs=[hbm] * 7,
        out_specs=(vmem, vmem),
        scratch_shapes=[
            pltpu.VMEM(query_in.shape, bf16),
            pltpu.VMEM(query_in.shape, bf16),
            pltpu.VMEM(query_out.shape, bf16),
            pltpu.VMEM(query_out.shape, bf16),
            pltpu.VMEM(eigvals.shape, bf16),
            pltpu.VMEM(out_basis.shape, bf16),
            pltpu.VMEM(in_basis.shape, bf16),
            pltpu.VMEM(eigvals.shape, f32),
            pltpu.VMEM((2, slots, own, depth), bf16),
            pltpu.VMEM((2, slots, own, across), bf16),
            pltpu.VMEM((2, 4, own, across), bf16),
            pltpu.VMEM((2, 4, own, across), bf16),
            pltpu.VMEM((2, 4, own, across), bf16),
            pltpu.VMEM((2, slots, own, across), bf16),
            pltpu.VMEM((2, slots, own, wide), bf16),
            pltpu.VMEM((2, slots, own, narrow), bf16),
            pltpu.VMEM((2, 4, own, narrow), bf16),
            pltpu.VMEM((2, 4, own, narrow), bf16),
            pltpu.VMEM((2, 4, own, narrow), bf16),
            pltpu.VMEM((2, slots, own, narrow), bf16),
            pltpu.VMEM((2, 8, kept), f32),
            pltpu.VMEM((4, 2, 8, kept), f32),
            pltpu.VMEM((4, 2, 8, kept), f32),
            pltpu.VMEM((3, 8, kept), f32),
            dma((11,)),
            dma((80,)),
            dma((2, 8)),
            dma((2, 4)),
            dma((2, 4)),
            dma((2, 8)),
            dma((2, 8)),
            dma((2, 3)),
            dma((9,)),
        ],
        compiler_params=pltpu.CompilerParams(
            collective_id=0, has_side_effects=True, vmem_limit_bytes=63 * 2**20
        ),
        cost_estimate=pl.CostEstimate(flops=4 * 10**9, bytes_accessed=10**7, transcendentals=0),
    )(query_out, query_in, out_basis, in_basis, eigvals, train_out, train_in)
    return (grad.astype(f32) / (eigvals + damping), scores.reshape(kept))


def fits(mesh):
    return dict(mesh.shape) == {"dp": 2, "row": 4, "col": 4}


def solution(mesh):
    in_specs = (
        P(("dp", "row"), "col"),
        P(("dp", "col"), None),
        P("col", ("dp", "row")),
        P(("dp", "row"), "col"),
        P(("dp", "row"), "col"),
        P(("dp", "row"), "col"),
        P(("dp", "col"), None),
    )
    out_specs = (P(("dp", "row"), "col"), P("dp"))
    return jax.shard_map(
        local_plan if fits(mesh) else wide_plan, mesh=mesh, in_specs=in_specs, out_specs=out_specs, check_vma=False
    )
```

```python
import functools

import jax
import jax.numpy as jnp
from jax import lax
from jax.experimental import pallas as pl
from jax.experimental.pallas import tpu as pltpu
from jax.sharding import PartitionSpec as P

damping = 1.0


def rotate_out(tok_rows, basis_panel):
    gathered = lax.all_gather(tok_rows, "row", axis=0, tiled=True)
    partial_sum = jnp.dot(gathered, basis_panel, preferred_element_type=jnp.float32)
    return lax.psum(partial_sum.astype(jnp.bfloat16), "col")


def rotate_in(tok_rows, basis_panel):
    groups = lax.axis_size("dp")
    row_count = lax.axis_size("row")
    sub_width = tok_rows.shape[1] // (groups * row_count)
    split_rows = tok_rows.reshape(tok_rows.shape[0], groups, row_count, sub_width)
    picked = lax.dynamic_index_in_dim(split_rows, lax.axis_index("row"), 2, keepdims=False)
    picked = picked.reshape(tok_rows.shape[0], groups * sub_width)
    gathered = lax.all_gather(picked, "col", axis=0, tiled=True)
    partial_sum = jnp.dot(gathered, basis_panel, preferred_element_type=jnp.float32)
    return lax.psum(partial_sum.astype(jnp.bfloat16), "row")


def wide_plan(query_out, query_in, out_basis, in_basis, eigvals, train_out, train_in):
    panel_out = lax.all_gather(out_basis, "dp", axis=1, tiled=True)
    panel_in = lax.all_gather(in_basis, "dp", axis=0, tiled=True)
    query_rot = rotate_out(query_out, panel_out)
    query_inr = rotate_in(query_in, panel_in)
    partial_grad = lax.dot_general(
        query_rot, query_inr, (((0,), (0,)), ((), ())), preferred_element_type=jnp.float32
    )
    owned = lax.psum_scatter(
        partial_grad.astype(jnp.bfloat16), "dp", scatter_dimension=0, tiled=True
    ).astype(jnp.float32)
    precond = owned / (eigvals + damping)
    shared = precond.astype(jnp.bfloat16)
    train_rot = rotate_out(train_out, panel_out)
    train_inr = rotate_in(train_in, panel_in)
    mixed = jnp.dot(
        train_rot,
        lax.all_gather(shared, "dp", axis=0, tiled=True),
        preferred_element_type=jnp.float32,
    )
    partial_scores = jnp.sum(mixed * train_inr.astype(jnp.float32), axis=1)
    scores = lax.psum(partial_scores, ("row", "col"))
    return (precond, scores)


bf16 = jnp.bfloat16
f32 = jnp.float32


def dot(left, right):
    return jnp.dot(left, right, preferred_element_type=f32)


def flat(block):
    return block.reshape(-1, block.shape[-1])


def kernel(
    q_out_hbm, q_in_hbm, basis_out_hbm, basis_in_hbm, eig_hbm, t_out_hbm, t_in_hbm,
    grad, scores,
    q_in, t_in, q_out, t_out, shared, basis_out, basis_in, eig, tin, pin, xr, zs, zr, fin, tout, pout, sr, ys, yr, rot,
    part, col_sc, row_sc, dp_sc,
    local_sem, send_sem, tin_sem, xr_sem, zr_sem, fin_sem, tout_sem, out_sem, sc_sem,
):
    d, r, c = lax.axis_index("dp"), lax.axis_index("row"), lax.axis_index("col")
    e = 1 - d
    core = lax.rem(c, 2)
    sib = c + 1 - 2 * core
    far = lax.rem(c + 2, 4)
    sibling, across, other = (d, r, sib), (d, r, far), (e, r, c)
    rows = [lax.rem(r + k, 4) for k in (1, 2, 3)]
    cols = [lax.rem(c + k, 4) for k in (1, 2, 3)]
    own_out, own_in, kept_row = 4 * d + r, 4 * d + c, 4 * e + r
    toks, outs = (q_in, t_in), (q_out, t_out)
    width = basis_in.shape[0]

    loads = [
        pltpu.make_async_copy(basis_in_hbm, basis_in, local_sem.at[0]),
        pltpu.make_async_copy(basis_out_hbm, basis_out, local_sem.at[1]),
        pltpu.make_async_copy(eig_hbm, eig, local_sem.at[2]),
    ]
    tokens = [
        pltpu.make_async_copy(src, dst, local_sem.at[7 + k])
        for k, (src, dst) in enumerate(
            ((q_in_hbm, q_in), (t_in_hbm, t_in), (q_out_hbm, q_out), (t_out_hbm, t_out))
        )
    ]
    for load in tokens + loads:
        load.start()

    barrier = pltpu.get_barrier_semaphore()
    peers = [(d, r, j) for j in cols] + [(d, j, c) for j in rows] + [other] + [(e, j, c) for j in rows]
    for peer in peers:
        pl.semaphore_signal(barrier, inc=1, device_id=peer, device_id_type=pl.DeviceIdType.MESH)
    pl.semaphore_wait(barrier, len(peers))

    sends = []

    def send(src, dst, sem, peer):
        copy = pltpu.make_async_remote_copy(
            src_ref=src, dst_ref=dst, send_sem=send_sem.at[len(sends)], recv_sem=sem,
            device_id=peer, device_id_type=pl.DeviceIdType.MESH,
        )
        copy.start()
        sends.append(copy)

    def got(dst, sem):
        pltpu.make_async_remote_copy(
            src_ref=dst, dst_ref=dst, send_sem=send_sem.at[0], recv_sem=sem,
            device_id=sibling, device_id_type=pl.DeviceIdType.MESH,
        ).wait_recv()

    def columns(ref, group):
        return ref.at[:, pl.ds(pl.multiple_of((group * 4 + r) * width, width), width)]

    mine, held = [], {}
    for ch in range(2):
        tokens[ch].wait()
        for peer in (other, across, sibling):
            send(columns(toks[ch], peer[0]), tin.at[ch, own_in], tin_sem.at[ch, own_in], peer)
        keep = pltpu.make_async_copy(columns(toks[ch], d), tin.at[ch, own_in], local_sem.at[3 + ch])
        keep.start()
        mine.append(keep)

    def spread_out(ch):
        tokens[2 + ch].wait()
        for j in rows:
            send(outs[ch], tout.at[ch, own_out], tout_sem.at[ch, own_out], (d, j, c))

        keep = pltpu.make_async_copy(outs[ch], tout.at[ch, own_out], local_sem.at[5 + ch])
        keep.start()
        held[ch] = keep

    sib_far = lax.rem(sib + 2, 4)

    def pass_tokens(ch, slot, targets):
        got(tin.at[ch, slot], tin_sem.at[ch, slot])
        for peer in targets:
            send(tin.at[ch, slot], tin.at[ch, slot], tin_sem.at[ch, slot], peer)

    def rotate_half(ch, half):
        for slot in (4 * half + sib, 4 * half + sib_far):
            got(tin.at[ch, slot], tin_sem.at[ch, slot])
        value = dot(flat(tin[ch, pl.ds(4 * half, 4)]), basis_in[...]).astype(bf16)
        pin[ch, pl.ds(4 * half, 4)] = value.reshape(4, -1, value.shape[-1])

    def rotate_own(ch):
        mine[ch].wait()
        if ch == 0:
            loads[0].wait()
        rotate_half(ch, d)
        for j in rows + [r]:
            send(pin.at[ch, 4 * d + j], xr.at[ch, j], xr_sem.at[ch, j], other)

    def scatter_rows(ch):
        for j in rows + [r]:
            got(xr.at[ch, j], xr_sem.at[ch, j])
            zs[ch, j] = (pin[ch, 4 * e + j].astype(f32) + xr[ch, j].astype(f32)).astype(bf16)
            if j is not r:
                send(zs.at[ch, j], zr.at[ch, r], zr_sem.at[ch, r], (d, j, c))

    def finish_piece(ch):
        total = zs[ch, r].astype(f32)
        for j in rows:
            got(zr.at[ch, j], zr_sem.at[ch, j])
            total = total + zr[ch, j].astype(f32)
        fin[ch, kept_row] = total.astype(bf16)
        for peer in [(d, j, c) for j in rows] + [other]:
            send(fin.at[ch, kept_row], fin.at[ch, kept_row], fin_sem.at[ch, kept_row], peer)

    def forward(buf, sem, ch, half):
        for j in rows:
            slot = 4 * half + j
            got(buf.at[ch, slot], sem.at[ch, slot])
            send(buf.at[ch, slot], buf.at[ch, slot], sem.at[ch, slot], other)

    def arrive(buf, sem, ch, half):
        for j in range(4):
            got(buf.at[ch, 4 * half + j], sem.at[ch, 4 * half + j])

    near, away = pl.ds(4 * core, 4), pl.ds(4 * (1 - core), 4)

    def rotate_out_part(ch):
        arrive(tout, tout_sem, ch, e)
        held[ch].wait()
        if ch == 0:
            loads[1].wait()
        for part_rows in (away, near):
            value = dot(flat(tout[ch, part_rows]), basis_out[...]).astype(bf16)
            pout[ch, part_rows] = value.reshape(4, -1, value.shape[-1])
            if part_rows is away:
                send(pout.at[ch, away], sr.at[ch], out_sem.at[ch, 0], sibling)

    def add_sibling(ch):
        got(sr.at[ch], out_sem.at[ch, 0])
        ys[ch] = (pout[ch, near].astype(f32) + sr[ch].astype(f32)).astype(bf16)
        send(ys.at[ch], yr.at[ch], out_sem.at[ch, 1], across)

    def add_across(ch):
        got(yr.at[ch], out_sem.at[ch, 1])
        rot[ch, near] = (ys[ch].astype(f32) + yr[ch].astype(f32)).astype(bf16)
        send(rot.at[ch, near], rot.at[ch, near], out_sem.at[ch, 2], sibling)

    def send_own_out(ch):
        send(outs[ch], tout.at[ch, own_out], tout_sem.at[ch, own_out], other)

    spread_out(0)
    send_own_out(0)
    spread_out(1)
    pass_tokens(0, 4 * d + far, [sibling])
    rotate_own(0)
    pass_tokens(1, 4 * d + far, [sibling])
    rotate_own(1)
    for ch in range(2):
        pass_tokens(ch, 4 * e + c, [across, sibling])
    for ch in range(2):
        pass_tokens(ch, 4 * e + far, [sibling])
    for ch in range(2):
        rotate_half(ch, e)
    scatter_rows(0)
    forward(tout, tout_sem, 0, d)
    scatter_rows(1)
    finish_piece(0)
    send_own_out(1)
    forward(tout, tout_sem, 1, d)
    rotate_out_part(0)
    add_sibling(0)
    finish_piece(1)
    forward(fin, fin_sem, 0, e)
    add_across(0)
    rotate_out_part(1)
    add_sibling(1)
    forward(fin, fin_sem, 1, e)
    add_across(1)

    arrive(fin, fin_sem, 0, d)
    got(rot.at[0, away], out_sem.at[0, 2])
    loads[2].wait()
    value = lax.dot_general(
        flat(rot[0]), flat(fin[0]), (((0,), (0,)), ((), ())), preferred_element_type=f32
    )
    grad[...] = value.astype(bf16)
    shared[...] = (value / (eig[...] + damping)).astype(bf16)

    got(rot.at[1, away], out_sem.at[1, 2])
    mixed = dot(flat(rot[1]), shared[...])
    arrive(fin, fin_sem, 1, d)
    product = mixed * flat(fin[1]).astype(f32)
    lanes = product[:, :128]
    for at in range(128, product.shape[1], 128):
        lanes = lanes + product[:, at:at + 128]
    line = jnp.sum(lanes.T, axis=0, keepdims=True)
    kept = line.shape[1] // 2
    part[0] = jnp.broadcast_to(line[:, :kept], part.shape[1:])
    part[1] = jnp.broadcast_to(line[:, kept:], part.shape[1:])

    col_sc[c] = part[...]
    for j in cols:
        send(part, col_sc.at[c], sc_sem.at[c], (d, r, j))
    for j in cols:
        got(col_sc.at[j], sc_sem.at[j])
    dp_sc[...] = ((col_sc[0] + col_sc[1]) + col_sc[2]) + col_sc[3]
    row_sc[own_out] = dp_sc[d]
    for half in (e, d):
        for j in rows + [r] if half is e else rows:
            send(dp_sc.at[half], row_sc.at[own_out], sc_sem.at[4 + own_out], (half, j, c))
    for half in (e, d):
        for j in rows + [r] if half is e else rows:
            got(row_sc.at[4 * half + j], sc_sem.at[4 + 4 * half + j])
    total = row_sc[0]
    for at in range(1, 8):
        total = total + row_sc[at]
    scores[...] = total[0:1]

    for copy in sends:
        copy.wait_send()


def local_plan(query_out, query_in, out_basis, in_basis, eigvals, train_out, train_in):
    own, wide = query_out.shape
    depth, across = in_basis.shape
    narrow = out_basis.shape[1]
    slots = lax.axis_size("dp") * lax.axis_size("row")
    kept = own * lax.axis_size("row")
    vmem = pl.BlockSpec(memory_space=pltpu.VMEM)
    hbm = pl.BlockSpec(memory_space=pl.ANY)
    dma = pltpu.SemaphoreType.DMA
    grad, scores = pl.pallas_call(
        kernel,
        out_shape=(
            jax.ShapeDtypeStruct(eigvals.shape, bf16),
            jax.ShapeDtypeStruct((1, kept), f32),
        ),
        in_specs=[hbm] * 7,
        out_specs=(vmem, vmem),
        scratch_shapes=[
            pltpu.VMEM(query_in.shape, bf16),
            pltpu.VMEM(query_in.shape, bf16),
            pltpu.VMEM(query_out.shape, bf16),
            pltpu.VMEM(query_out.shape, bf16),
            pltpu.VMEM(eigvals.shape, bf16),
            pltpu.VMEM(out_basis.shape, bf16),
            pltpu.VMEM(in_basis.shape, bf16),
            pltpu.VMEM(eigvals.shape, f32),
            pltpu.VMEM((2, slots, own, depth), bf16),
            pltpu.VMEM((2, slots, own, across), bf16),
            pltpu.VMEM((2, 4, own, across), bf16),
            pltpu.VMEM((2, 4, own, across), bf16),
            pltpu.VMEM((2, 4, own, across), bf16),
            pltpu.VMEM((2, slots, own, across), bf16),
            pltpu.VMEM((2, slots, own, wide), bf16),
            pltpu.VMEM((2, slots, own, narrow), bf16),
            pltpu.VMEM((2, 4, own, narrow), bf16),
            pltpu.VMEM((2, 4, own, narrow), bf16),
            pltpu.VMEM((2, 4, own, narrow), bf16),
            pltpu.VMEM((2, slots, own, narrow), bf16),
            pltpu.VMEM((2, 8, kept), f32),
            pltpu.VMEM((4, 2, 8, kept), f32),
            pltpu.VMEM((slots, 8, kept), f32),
            pltpu.VMEM((2, 8, kept), f32),
            dma((11,)),
            dma((80,)),
            dma((2, 8)),
            dma((2, 4)),
            dma((2, 4)),
            dma((2, 8)),
            dma((2, 8)),
            dma((2, 3)),
            dma((12,)),
        ],
        compiler_params=pltpu.CompilerParams(
            collective_id=0, has_side_effects=True, vmem_limit_bytes=63 * 2**20
        ),
        cost_estimate=pl.CostEstimate(flops=4 * 10**9, bytes_accessed=10**7, transcendentals=0),
    )(query_out, query_in, out_basis, in_basis, eigvals, train_out, train_in)
    return (grad.astype(f32) / (eigvals + damping), scores.reshape(kept))


def fits(mesh):
    return dict(mesh.shape) == {"dp": 2, "row": 4, "col": 4}


def solution(mesh):
    in_specs = (
        P(("dp", "row"), "col"),
        P(("dp", "col"), None),
        P("col", ("dp", "row")),
        P(("dp", "row"), "col"),
        P(("dp", "row"), "col"),
        P(("dp", "row"), "col"),
        P(("dp", "col"), None),
    )
    out_specs = (P(("dp", "row"), "col"), P("dp"))
    return jax.shard_map(
        local_plan if fits(mesh) else wide_plan, mesh=mesh, in_specs=in_specs, out_specs=out_specs, check_vma=False
    )
```
